768 devices in a mesh: tile: 96 (over z, y), spec: 8 (over x, core).
Axes of the slice: x: 4, y: 8, z: 12, core: 2. Of those that a mesh axis runs over, the one named last changes fastest.
Arguments:
- spectra: float32 [864, 768, 128], P('spec', 'tile'), may hold values from 0.05 to 2
- wind_speed: float32 [768, 128], P('tile'), may hold values from 3 to 20
- wind_dir: float32 [768, 128], P('tile'), may hold values from -3.140625 to 3.140625
- sea_mask: int32 [768, 128], P('tile'), may hold values 0 or 1
- neighbours: int32 [768, 4], P('tile'), may hold values from -1 to 767, as said below
Outputs:
- spectra_next: float32 [864, 768, 128], P('spec', 'tile')
The draws below stay inside these ranges and needn't reach their ends.
Inputs may be any that keep to these rules, and one draw needn't show every extreme that they name: Tiles come in aligned blocks of 8; block b is one row of the basin's tiles in shuffled order. A tile's north neighbour lies in block b - 1, its south neighbour in block b + 1, its west and east neighbours in block b; the relations are mutual (my north's south is me, my west's east is me). Block 0 has no north neighbours, the last block no south ones, one tile of each block no west neighbour and one no east neighbour.
All inputs are finite; a program needn't handle non-finite values. No bound on the sum of `sea_mask` on one device may be relied on, other than what follows from the above.
Results may differ from the reference program's by a relative error of at most 0.0003.
Values sent between devices are 32-bit elements; how exact they have to be, the bound alone decides.
A program may use at most 32 MiB of HBM per device.

```python
import math
import jax
import jax.numpy as jnp
from jax import lax

NFREQ = 24
NDIR = 36
ROWS = 4
COLS = 32
SUBSTEPS = 4
SOURCE_ITERS = 3
TILES_DEV = 8
TILE_POINTS = 128
COMPONENTS = 864
TILES = 768


def draw_neighbours(key, part):
    key = jax.random.fold_in(key, 11)
    count_rows = TILES // TILES_DEV
    keys = jax.random.split(key, count_rows)
    column = jax.vmap(lambda k: jax.random.permutation(k, TILES_DEV))(keys).astype(jnp.int32)
    inverse = jnp.argsort(column, axis=1).astype(jnp.int32)
    row_index = jnp.arange(count_rows, dtype=jnp.int32)[:, None]
    inverse_up = jnp.roll(inverse, 1, axis=0)
    inverse_down = jnp.roll(inverse, -1, axis=0)
    north = jnp.where(row_index > 0, (row_index - 1) * TILES_DEV + jnp.take_along_axis(inverse_up, column, axis=1), -1)
    south = jnp.where(row_index < count_rows - 1, (row_index + 1) * TILES_DEV + jnp.take_along_axis(inverse_down, column, axis=1), -1)
    west_slot = jnp.take_along_axis(inverse, jnp.maximum(column - 1, 0), axis=1)
    east_slot = jnp.take_along_axis(inverse, jnp.minimum(column + 1, TILES_DEV - 1), axis=1)
    west = jnp.where(column > 0, row_index * TILES_DEV + west_slot, -1)
    east = jnp.where(column < TILES_DEV - 1, row_index * TILES_DEV + east_slot, -1)
    stacked = jnp.stack([north, south, west, east], axis=-1)
    return stacked.reshape(TILES, 4).astype(jnp.int32)


def set_ends(result, key, low, top_value):
    shape = result.shape
    index_at = [jax.random.randint(jax.random.fold_in(key, axis), (), 0, shape[axis]) for axis in range(len(shape))]
    result = result.at[tuple(index_at)].set(low)
    longest = shape.index(max(shape))
    index_at[longest] = (index_at[longest] + 1) % shape[longest]
    return result.at[tuple(index_at)].set(top_value)


def shard_levels(key, extent, cuts, least, high):
    loudness = 1.0
    for axis_at, blocks in cuts:
        draws = jax.random.uniform(jax.random.fold_in(jax.random.fold_in(key, 6), axis_at), (blocks,), jnp.float32, least / len(cuts), high / len(cuts))
        loudness = loudness * jnp.repeat(jnp.exp(draws), extent[axis_at] // blocks).reshape((-1,) + (1,) * (len(extent) - 1 - axis_at))
    return loudness


def setup_inputs(seed: int = 0) -> dict:
    streams_of = jax.random.split(jax.random.key(seed), 6)
    spectra = jnp.clip(jnp.exp(math.log(2.0) - 3.6888794 * jax.random.uniform(streams_of[0], (COMPONENTS, TILES, TILE_POINTS), jnp.float32) ** shard_levels(streams_of[0], (COMPONENTS, TILES, TILE_POINTS), ((0, 8), (1, 96)), -0.2, 0.2)), 0.05, 2.0)
    wind_speed = jnp.clip(3.0 + 17.0 * jax.random.uniform(streams_of[1], (TILES, TILE_POINTS), jnp.float32) ** shard_levels(streams_of[1], (TILES, TILE_POINTS), ((0, 96),), -0.2, 0.2), 3.0, 20.0)
    wind_dir = jnp.clip(jax.random.uniform(streams_of[2], (TILES, TILE_POINTS), jnp.float32, -3.140625, 3.140625), -3.140625, 3.140625)
    sea_mask = set_ends((jax.random.randint(streams_of[3], (TILES, TILE_POINTS), 0, 8) < 7).astype(jnp.int32), jax.random.fold_in(streams_of[3], 1), 0, 1)
    neighbours = draw_neighbours(jax.random.fold_in(streams_of[5], 71), 0)
    return dict(spectra=spectra, wind_speed=wind_speed, wind_dir=wind_dir, sea_mask=sea_mask, neighbours=neighbours)


def comp_tables(first, count):
    index = first + jnp.arange(count, dtype=jnp.int32)
    freq_index = (index // NDIR).astype(jnp.float32)
    direction = ((index % NDIR).astype(jnp.float32) + 0.5) * (2.0 * math.pi / NDIR)
    ratio = jnp.power(jnp.float32(1.1), freq_index)
    speed = 0.65 / ratio
    return (ratio, direction, speed * jnp.cos(direction), speed * jnp.sin(direction))

def advect(energy, north_rim, south_rim, west_col, east_col, east_speed, south_speed, sea):
    above = jnp.concatenate([north_rim[:, :, None, :], energy[:, :, :-1, :]], axis=2)
    beneath = jnp.concatenate([energy[:, :, 1:, :], south_rim[:, :, None, :]], axis=2)
    leftward = jnp.concatenate([west_col[:, :, :, None], energy[:, :, :, :-1]], axis=3)
    rightward = jnp.concatenate([energy[:, :, :, 1:], east_col[:, :, :, None]], axis=3)
    upwind_x = jnp.where(east_speed > 0, leftward, rightward)
    upwind_y = jnp.where(south_speed > 0, above, beneath)
    moved = energy - jnp.abs(east_speed) * (energy - upwind_x) - jnp.abs(south_speed) * (energy - upwind_y)
    return moved * sea[None]

def moment_terms(energy, ratio):
    return (lax.optimization_barrier(jnp.sum(ratio * energy, axis=0)), lax.optimization_barrier(jnp.sum(ratio * ratio * energy, axis=0)))

def source_step(energy, total, weighted, ratio, direction, speed_w, dir_w, sea):
    first_moment = total / COMPONENTS
    second_moment = weighted / COMPONENTS
    mean_ratio = (second_moment + 0.1) / (first_moment + 0.1)
    cosine = jnp.cos(direction - dir_w[None])
    grow = 0.03 * speed_w[None] * jnp.maximum(cosine, 0.0) * jnp.sqrt(ratio)
    damp = 0.25 * first_moment[None] * jnp.square(ratio / mean_ratio[None])
    change = 0.2 * (grow - damp) * energy
    limit = 0.08 / ratio
    change = jnp.clip(change, -limit, limit)
    return jnp.maximum(energy + change, 0.0) * sea[None]

def lookup(rows, ids):
    valid = (ids >= 0).astype(jnp.float32)
    return jnp.take(rows, jnp.maximum(ids, 0), axis=1) * valid[None, :, None]

def reference(spectra, wind_speed, wind_dir, sea_mask, neighbours):
    sea_flat = sea_mask.astype(jnp.float32)
    sea = sea_flat.reshape(TILES, ROWS, COLS)
    energy = spectra.reshape(NFREQ, NDIR, TILES, ROWS, COLS) * sea[None, None]
    north_ids = neighbours[:, 0]
    south_ids = neighbours[:, 1]
    west_ids = neighbours[:, 2]
    east_ids = neighbours[:, 3]

    def propagate(inputs):
        block, freq = inputs
        ratio, direction, east_speed, south_speed = comp_tables(freq * NDIR, NDIR)
        east_speed = east_speed[:, None, None, None]
        south_speed = south_speed[:, None, None, None]
        for step in range(SUBSTEPS):
            north_rim = lookup(block[:, :, ROWS - 1, :], north_ids)
            south_rim = lookup(block[:, :, 0, :], south_ids)
            west_col = lookup(block[:, :, :, COLS - 1], west_ids)
            east_col = lookup(block[:, :, :, 0], east_ids)
            block = advect(block, north_rim, south_rim, west_col, east_col, east_speed, south_speed, sea)
        return block
    moved = lax.map(propagate, (energy, jnp.arange(NFREQ, dtype=jnp.int32)))
    groups = TILES // TILES_DEV
    blocks = moved.reshape(COMPONENTS, groups, TILES_DEV, TILE_POINTS).transpose(1, 0, 2, 3)
    speed_blocks = wind_speed.reshape(groups, TILES_DEV, TILE_POINTS)
    dir_blocks = wind_dir.reshape(groups, TILES_DEV, TILE_POINTS)
    sea_blocks = sea_flat.reshape(groups, TILES_DEV, TILE_POINTS)
    ratio, direction, unused_east, unused_south = comp_tables(0, COMPONENTS)
    ratio = ratio[:, None, None]
    direction = direction[:, None, None]

    def relax(inputs):
        block, speed_w, dir_w, sea_w = inputs
        for step in range(SOURCE_ITERS):
            total, weighted = moment_terms(block, ratio)
            block = source_step(block, total, weighted, ratio, direction, speed_w, dir_w, sea_w)
        return block
    relaxed = lax.map(relax, (blocks, speed_blocks, dir_blocks, sea_blocks))
    return relaxed.transpose(1, 0, 2, 3).reshape(COMPONENTS, TILES, TILE_POINTS)
```

```python
import functools
import math

import jax
import jax.numpy as jnp
import numpy as np
from jax import lax
from jax.experimental import pallas as pl
from jax.experimental.pallas import tpu as pltpu
from jax.sharding import PartitionSpec as P

NDIR = 36
ROWS = 4
COLS = 32
SUBSTEPS = 4
SOURCE_ITERS = 3
QUAD = 9
POINTS = ROWS * COLS
MESH = pl.DeviceIdType.MESH

ANGLE = (np.arange(NDIR) + 0.5) * (2.0 * math.pi / NDIR)


def table_pick(index, values):
    out = jnp.float32(values[0])
    for k in range(1, len(values)):
        out = jnp.where(index == k, jnp.float32(values[k]), out)
    return out


def take_rows(x, index):
    return jnp.take_along_axis(x, index, axis=0)


def take_lanes(x, index):
    return jnp.take_along_axis(x, index, axis=1)


def kernel(
    nt, ns, nf,
    spectra, speed_hbm, dir_hbm, mask_hbm, nb_hbm, out,
    own, halo, nb, small_f, small_i, aux_out, aux_in, grow, part, moments,
    load_sem, small_sem, aux_send, aux_recv, halo_send, halo_recv, mom_send, mom_recv, out_sem,
):
    tile = lax.axis_index("tile")
    spec = lax.axis_index("spec")
    above, beneath = lax.rem(tile + nt - 1, nt), lax.rem(tile + 1, nt)
    tiles_dev = own.shape[1]
    comps = nf * NDIR
    total_comps = comps * ns
    half = NDIR // 2

    barrier = pltpu.get_barrier_semaphore()
    for other in (above, beneath):
        pl.semaphore_signal(barrier, inc=1, device_id={"tile": other}, device_id_type=MESH)
    for k in range(1, ns):
        pl.semaphore_signal(
            barrier, inc=1, device_id={"spec": lax.rem(spec + k, ns)}, device_id_type=MESH
        )

    small = [
        pltpu.make_async_copy(nb_hbm, nb, small_sem.at[0]),
        pltpu.make_async_copy(mask_hbm, small_i, small_sem.at[1]),
        pltpu.make_async_copy(speed_hbm, small_f.at[0], small_sem.at[2]),
        pltpu.make_async_copy(dir_hbm, small_f.at[1], small_sem.at[3]),
    ]
    for copy in small:
        copy.start()
    loads = [
        pltpu.make_async_copy(
            spectra.at[pl.ds(lf * NDIR, NDIR)], own.at[pl.ds(lf * NDIR, NDIR)], load_sem.at[lf]
        )
        for lf in range(nf)
    ]
    for copy in loads:
        copy.start()

    shape = (tiles_dev, POINTS)
    lane = lax.broadcasted_iota(jnp.int32, shape, 1)
    row_of = lane // COLS
    col_of = lane - row_of * COLS
    sublane = lax.broadcasted_iota(jnp.int32, shape, 0)
    small[0].wait()
    ids = nb[...]
    base = tile * tiles_dev

    def spread(k):
        return jnp.broadcast_to(ids[:, k : k + 1], shape)

    def local(wide, first):
        return jnp.clip(wide - first, 0, tiles_dev - 1)

    north_id, south_id, west_id, east_id = [spread(k) for k in range(4)]
    north_at, south_at = local(north_id, base - tiles_dev), local(south_id, base + tiles_dev)
    west_at, east_at = local(west_id, base), local(east_id, base)
    small[1].wait()
    mask_i = small_i[...]
    for way, place in ((0, south_at), (1, north_at)):
        aux_out[way, 0] = mask_i
        aux_out[way, 1] = jnp.where(west_id >= 0, take_rows(place, west_at), -1)
        aux_out[way, 2] = jnp.where(east_id >= 0, take_rows(place, east_at), -1)

    pl.semaphore_wait(barrier, 2 + ns - 1)

    sends = []
    for way, other in ((0, beneath), (1, above)):
        sends.append(
            pltpu.make_async_remote_copy(
                src_ref=aux_out.at[way], dst_ref=aux_in.at[way],
                send_sem=aux_send.at[way], recv_sem=aux_recv.at[way],
                device_id={"tile": other}, device_id_type=MESH,
            )
        )
    for lf in range(nf):
        for q in range(2):
            for way, other in ((0, beneath), (1, above)):
                run = pl.ds(lf * NDIR + way * half + q * QUAD, QUAD)
                slot = lf * 4 + way * 2 + q
                sends.append(
                    pltpu.make_async_remote_copy(
                        src_ref=spectra.at[run], dst_ref=halo.at[run],
                        send_sem=halo_send.at[slot], recv_sem=halo_recv.at[slot],
                        device_id={"tile": other}, device_id_type=MESH,
                    )
                )
    for copy in sends:
        copy.start()

    small[2].wait()
    small[3].wait()
    scaled = small_f[0] * jnp.float32(0.2 * 0.03)
    cos_w, sin_w = jnp.cos(small_f[1]), jnp.sin(small_f[1])
    for d in range(NDIR):
        cosine = cos_w * jnp.float32(math.cos(ANGLE[d])) + sin_w * jnp.float32(math.sin(ANGLE[d]))
        grow[d] = scaled * jnp.maximum(cosine, 0.0)

    mask = mask_i.astype(jnp.float32)
    one = jnp.float32(1.0)
    zero = jnp.float32(0.0)

    def sideways(at, valid, edge):
        return (
            jnp.where(col_of == edge, at, sublane),
            jnp.where((col_of == COLS - 1 - edge) & jnp.logical_not(valid), zero, one),
        )

    from_west = row_of * COLS + lax.rem(col_of + COLS - 1, COLS)
    from_east = row_of * COLS + lax.rem(col_of + 1, COLS)
    side_own = (
        sideways(west_at, west_id >= 0, COLS - 1),
        sideways(east_at, east_id >= 0, 0),
    )
    lanes_of = (from_west, from_east)
    ratio_spec = table_pick(spec, [1.1 ** (nf * s) for s in range(ns)])
    ratio_of = [ratio_spec * jnp.float32(1.1**lf) for lf in range(nf)]

    aux_waits = sends[:2]
    for copy in aux_waits:
        copy.wait_recv()
    halo_setup = []
    for way, (place, ident) in enumerate(((north_at, north_id), (south_at, south_id))):
        hmask = jnp.where(ident >= 0, take_rows(aux_in[way, 0], place), 0).astype(jnp.float32)
        sides = []
        for k, edge in ((1, COLS - 1), (2, 0)):
            at = take_rows(aux_in[way, k], place)
            sides.append(sideways(jnp.maximum(at, 0), at >= 0, edge))
        halo_setup.append((hmask, sides))

    def advance_freq(lf, carry):
        first, second = carry
        ratio = jnp.float32(ratio_of[0])
        for k in range(1, nf):
            ratio = jnp.where(lf == k, ratio_of[k], ratio)
        speed = jnp.float32(0.65) / ratio
        subtotal = jnp.zeros(shape, jnp.float32)
        start = lf * NDIR
        pltpu.make_async_copy(
            spectra.at[pl.ds(start, NDIR)], own.at[pl.ds(start, NDIR)], load_sem.at[lf]
        ).wait()
        for q, way, side in ((0, 0, 0), (0, 1, 1), (1, 0, 1), (1, 1, 0)):
            run = pl.ds(start + way * half + q * QUAD, QUAD)
            slot = lf * 4 + way * 2 + q
            pltpu.make_async_remote_copy(
                src_ref=spectra.at[run], dst_ref=halo.at[run],
                send_sem=halo_send.at[slot], recv_sem=halo_recv.at[slot],
                device_id={"tile": beneath if way == 0 else above}, device_id_type=MESH,
            ).wait_recv()
            place = north_at if way == 0 else south_at
            inner = ROWS - 1 if way == 0 else 0
            turn = COLS if way == 0 else POINTS - COLS
            rim = row_of == inner
            hmask, hsides = halo_setup[way]
            pull, keep = side_own[side]
            hpull, hkeep = hsides[side]
            lanes = lanes_of[side]
            for i in range(QUAD):
                d = way * half + q * QUAD + i
                ax = speed * jnp.float32(abs(math.cos(ANGLE[d])))
                ay = speed * jnp.float32(abs(math.sin(ANGLE[d])))
                rest = one - ax - ay
                kx, hkx = keep * ax, hkeep * ax
                x = own[start + d] * mask
                h = take_rows(halo[start + d], place) * hmask
                for step in range(SUBSTEPS):
                    side_x = take_lanes(take_rows(x, pull), lanes)
                    side_y = pltpu.roll(jnp.where(rim, h, x), turn, 1)
                    x = (rest * x + kx * side_x + ay * side_y) * mask
                    if step < SUBSTEPS - 1:
                        side_x = take_lanes(take_rows(h, hpull), lanes)
                        side_y = pltpu.roll(h, turn, 1)
                        h = (rest * h + hkx * side_x + ay * side_y) * hmask
                own[start + d] = x
                subtotal = subtotal + x
        weighted = ratio * subtotal
        return first + weighted, second + ratio * weighted

    empty = jnp.zeros(shape, jnp.float32)
    first, second = lax.fori_loop(0, nf, advance_freq, (empty, empty))

    chunk = NDIR // 3
    for step in range(SOURCE_ITERS):
        part[step, 0] = first
        part[step, 1] = second
        passes = []
        for k in range(1, ns):
            passes.append(
                pltpu.make_async_remote_copy(
                    src_ref=part.at[step], dst_ref=moments.at[step, k - 1],
                    send_sem=mom_send.at[step, k - 1], recv_sem=mom_recv.at[step, k - 1],
                    device_id={"spec": lax.rem(spec + k, ns)}, device_id_type=MESH,
                )
            )
        for copy in passes:
            copy.start()
        sends.extend(passes)
        for k in range(1, ns):
            passes[k - 1].wait_recv()
            first = first + moments[step, k - 1, 0]
            second = second + moments[step, k - 1, 1]
        first = first * jnp.float32(1.0 / total_comps)
        second = second * jnp.float32(1.0 / total_comps)
        mean_ratio = (second + 0.1) / (first + 0.1)
        damping = jnp.float32(0.2 * 0.25) * first / (mean_ratio * mean_ratio)
        damp = [damping * (ratio * ratio) for ratio in ratio_of]
        root = [ratio_spec_root * jnp.float32(math.sqrt(1.1**lf)) for lf in range(nf)
                for ratio_spec_root in (table_pick(spec, [math.sqrt(1.1 ** (nf * s)) for s in range(ns)]),)]
        limit = [jnp.float32(0.08) / ratio for ratio in ratio_of]

        def relax(j, sums):
            sums = list(sums)
            for i in range(chunk):
                d = j * chunk + i
                g = grow[d]
                for lf in range(nf):
                    x = own[lf * NDIR + d]
                    change = (g * root[lf] - damp[lf]) * x
                    change = jnp.minimum(jnp.maximum(change, -limit[lf]), limit[lf])
                    x = jnp.maximum(x + change, 0.0) * mask
                    own[lf * NDIR + d] = x
                    sums[lf] = sums[lf] + x
            if step == SOURCE_ITERS - 1:
                for lf in range(nf):
                    run = pl.ds(lf * NDIR + j * chunk, chunk)
                    pltpu.make_async_copy(own.at[run], out.at[run], out_sem.at[j, lf]).start()
            return tuple(sums)

        sums = lax.fori_loop(0, NDIR // chunk, relax, (empty,) * nf)
        first = sum(ratio * s for ratio, s in zip(ratio_of, sums))
        second = sum(ratio * ratio * s for ratio, s in zip(ratio_of, sums))

    for j in range(NDIR // chunk):
        for lf in range(nf):
            run = pl.ds(lf * NDIR + j * chunk, chunk)
            pltpu.make_async_copy(own.at[run], out.at[run], out_sem.at[j, lf]).wait()
    for copy in sends:
        copy.wait_send()


def body(nt, ns, spectra, wind_speed, wind_dir, sea_mask, neighbours):
    comps, tiles_dev, points = spectra.shape
    nf = comps // NDIR
    anywhere = pl.BlockSpec(memory_space=pl.ANY)
    dma = pltpu.SemaphoreType.DMA
    return pl.pallas_call(
        functools.partial(kernel, nt, ns, nf),
        out_shape=jax.ShapeDtypeStruct(spectra.shape, jnp.float32),
        in_specs=[anywhere] * 5,
        out_specs=anywhere,
        scratch_shapes=[
            pltpu.VMEM((comps, tiles_dev, points), jnp.float32),
            pltpu.VMEM((comps, tiles_dev, points), jnp.float32),
            pltpu.VMEM((tiles_dev, 4), jnp.int32),
            pltpu.VMEM((2, tiles_dev, points), jnp.float32),
            pltpu.VMEM((tiles_dev, points), jnp.int32),
            pltpu.VMEM((2, 3, tiles_dev, points), jnp.int32),
            pltpu.VMEM((2, 3, tiles_dev, points), jnp.int32),
            pltpu.VMEM((NDIR, tiles_dev, points), jnp.float32),
            pltpu.VMEM((SOURCE_ITERS, 2, tiles_dev, points), jnp.float32),
            pltpu.VMEM((SOURCE_ITERS, ns - 1, 2, tiles_dev, points), jnp.float32),
            dma((nf,)),
            dma((4,)),
            dma((2,)),
            dma((2,)),
            dma((nf * 4,)),
            dma((nf * 4,)),
            dma((SOURCE_ITERS, ns - 1)),
            dma((SOURCE_ITERS, ns - 1)),
            dma((3, nf)),
        ],
        compiler_params=pltpu.CompilerParams(
            collective_id=0, has_side_effects=True, vmem_limit_bytes=16 * 1024 * 1024
        ),
    )(spectra, wind_speed, wind_dir, sea_mask, neighbours)


def solution(mesh):
    placed = (
        P("spec", "tile", None),
        P("tile", None),
        P("tile", None),
        P("tile", None),
        P("tile", None),
    )
    return jax.shard_map(
        functools.partial(body, mesh.shape["tile"], mesh.shape["spec"]),
        mesh=mesh, in_specs=placed, out_specs=P("spec", "tile", None), check_vma=False,
    )
```

```python
import functools
import math

import jax
import jax.numpy as jnp
import numpy as np
from jax import lax
from jax.experimental import pallas as pl
from jax.experimental.pallas import tpu as pltpu
from jax.sharding import PartitionSpec as P

NDIR = 36
ROWS = 4
COLS = 32
SUBSTEPS = 4
SOURCE_ITERS = 3
QUAD = 9
POINTS = ROWS * COLS
MESH = pl.DeviceIdType.MESH

ANGLE = (np.arange(NDIR) + 0.5) * (2.0 * math.pi / NDIR)


def table_pick(index, values):
    out = jnp.float32(values[0])
    for k in range(1, len(values)):
        out = jnp.where(index == k, jnp.float32(values[k]), out)
    return out


def table_rows(row, values):
    out = jnp.full(row.shape, values[0], jnp.float32)
    for k in range(1, len(values)):
        out = jnp.where(row == k, jnp.float32(values[k]), out)
    return out


def take_rows(x, index):
    return jnp.take_along_axis(x, index, axis=0)


def take_lanes(x, index):
    return jnp.take_along_axis(x, index, axis=1)


def kernel(
    nt, ns, nf,
    spectra, speed_hbm, dir_hbm, mask_hbm, nb_hbm, own,
    halo, nb, small_f, small_i, aux_out, aux_in, grow, grow_row, gathered, q_out, q_in,
    index_t, factor_t,
    load_sem, small_sem, aux_send, aux_recv, halo_send, halo_recv,
    share_send, share_recv, share_own, q_send, q_recv,
):
    tile = lax.axis_index("tile")
    spec = lax.axis_index("spec")
    above, beneath = jnp.maximum(tile - 1, 0), jnp.minimum(tile + 1, nt - 1)
    tiles_dev = own.shape[1]
    comps = nf * NDIR
    total_comps = comps * ns
    blocks = nf * ns // 8
    half = NDIR // 2

    barrier = pltpu.get_barrier_semaphore()
    ways = ((0, beneath, tile < nt - 1), (1, above, tile > 0))
    for way, other, there in ways:

        @pl.when(there)
        def _():
            pl.semaphore_signal(barrier, inc=1, device_id={"tile": other}, device_id_type=MESH)

    for k in range(1, ns):
        pl.semaphore_signal(
            barrier, inc=1, device_id={"spec": lax.rem(spec + k, ns)}, device_id_type=MESH
        )

    small = [
        pltpu.make_async_copy(nb_hbm, nb, small_sem.at[0]),
        pltpu.make_async_copy(mask_hbm, small_i, small_sem.at[1]),
        pltpu.make_async_copy(speed_hbm, small_f.at[0], small_sem.at[2]),
        pltpu.make_async_copy(dir_hbm, small_f.at[1], small_sem.at[3]),
    ]
    for copy in small:
        copy.start()

    def own_copy(lf):
        run = pl.ds(lf * NDIR, NDIR)
        return pltpu.make_async_copy(spectra.at[run], own.at[run], load_sem.at[lf])

    for lf in range(nf):
        own_copy(lf).start()

    def aux_copy(way, other):
        return pltpu.make_async_remote_copy(
            src_ref=aux_out.at[way], dst_ref=aux_in.at[way],
            send_sem=aux_send.at[way], recv_sem=aux_recv.at[way],
            device_id={"tile": other}, device_id_type=MESH,
        )

    def halo_copy(lf, way, other):
        run = pl.ds(lf * NDIR + way * half, half)
        return pltpu.make_async_remote_copy(
            src_ref=spectra.at[run], dst_ref=halo.at[run],
            send_sem=halo_send.at[lf, way], recv_sem=halo_recv.at[lf, way],
            device_id={"tile": other}, device_id_type=MESH,
        )

    pl.semaphore_wait(
        barrier, ns - 1 + (tile > 0).astype(jnp.int32) + (tile < nt - 1).astype(jnp.int32)
    )
    comes = (tile > 0, tile < nt - 1)
    for way, other, there in ways:

        @pl.when(there)
        def _():
            halo_copy(0, way, other).start()

    shape = (tiles_dev, POINTS)
    lane = lax.broadcasted_iota(jnp.int32, shape, 1)
    row_of = lane // COLS
    col_of = lane - row_of * COLS
    sublane = lax.broadcasted_iota(jnp.int32, shape, 0)
    small[0].wait()
    base = tile * tiles_dev

    def spread(k):
        wide = jnp.full(shape, nb[k, 0], jnp.int32)
        for s in range(1, tiles_dev):
            wide = jnp.where(sublane == s, nb[k, s], wide)
        return wide

    def local(wide, first):
        return jnp.clip(wide - first, 0, tiles_dev - 1)

    north_id, south_id, west_id, east_id = [spread(k) for k in range(4)]
    north_at, south_at = local(north_id, base - tiles_dev), local(south_id, base + tiles_dev)
    west_at, east_at = local(west_id, base), local(east_id, base)
    small[1].wait()
    mask_i = small_i[...]
    for way, place in ((0, south_at), (1, north_at)):
        aux_out[way, 0] = mask_i
        aux_out[way, 1] = jnp.where(west_id >= 0, take_rows(place, west_at), -1)
        aux_out[way, 2] = jnp.where(east_id >= 0, take_rows(place, east_at), -1)

    for way, other, there in ways:

        @pl.when(there)
        def _():
            aux_copy(way, other).start()

        @pl.when(jnp.logical_not(comes[way]))
        def _():
            aux_in[way] = jnp.zeros(aux_in.shape[1:], jnp.int32)
            for lf in range(nf):
                run = pl.ds(lf * NDIR + way * half, half)
                halo[run] = jnp.zeros((half,) + shape, jnp.float32)

    def next_halo(lf):
        for way, other, there in ways:

            @pl.when(there)
            def _():
                halo_copy(lf - 1, way, other).wait_send()
                halo_copy(lf, way, other).start()

    small[2].wait()
    small[3].wait()
    scaled = small_f[0] * jnp.float32(0.2 * 0.03)
    small_f[2] = jnp.cos(small_f[1])
    small_f[3] = jnp.sin(small_f[1])
    small_f[4] = mask_i.astype(jnp.float32)
    small_f[5] = scaled

    def mine(k):
        return jnp.broadcast_to(small_f[k, pl.ds(spec, 1), :], (8, POINTS))

    for target, cos_w, sin_w, scale in (
        (grow, small_f[2], small_f[3], scaled), (grow_row, mine(2), mine(3), mine(5))
    ):
        for d in range(NDIR):
            cosine = cos_w * jnp.float32(math.cos(ANGLE[d]))
            cosine = cosine + sin_w * jnp.float32(math.sin(ANGLE[d]))
            target[d] = scale * jnp.maximum(cosine, 0.0)
    for lf in range(1, nf):
        next_halo(lf)

    mask = mask_i.astype(jnp.float32)
    one = jnp.float32(1.0)
    zero = jnp.float32(0.0)
    empty = jnp.zeros(shape, jnp.float32)
    ratio_spec = table_pick(spec, [1.1 ** (nf * s) for s in range(ns)])
    ratio_of = [ratio_spec * jnp.float32(1.1**lf) for lf in range(nf)]

    def sideways(at, valid, edge):
        return (
            jnp.where(col_of == edge, at, sublane),
            jnp.where((col_of == COLS - 1 - edge) & jnp.logical_not(valid), zero, one),
        )

    lanes_of = (
        row_of * COLS + lax.rem(col_of + COLS - 1, COLS),
        row_of * COLS + lax.rem(col_of + 1, COLS),
    )
    side_own = (
        sideways(west_at, west_id >= 0, COLS - 1),
        sideways(east_at, east_id >= 0, 0),
    )
    for way, place, ident, turn in (
        (0, north_at, north_id, POINTS - COLS), (1, south_at, south_id, COLS)
    ):

        @pl.when(comes[way])
        def _():
            aux_copy(way, ways[way][1]).wait_recv()

        factor_t[way, 4] = jnp.where(ident >= 0, take_rows(aux_in[way, 0], place), 0).astype(
            jnp.float32
        )
        index_t[way, 6] = place
        index_t[way, 7] = lax.rem(lane + turn, POINTS)
        for q in range(2):
            side = way if q == 0 else 1 - way
            pull, keep = side_own[side]
            at = take_rows(aux_in[way, 1 + side], place)
            hpull, hkeep = sideways(jnp.maximum(at, 0), at >= 0, COLS - 1 if side == 0 else 0)
            index_t[way, q], index_t[way, 2 + q], index_t[way, 4 + q] = pull, hpull, lanes_of[side]
            factor_t[way, q], factor_t[way, 2 + q] = keep, hkeep

    chunk = NDIR // 3
    order = sorted(range(1, ns), key=lambda k: -min(k // 2, (ns - k) // 2))

    def peer(k):
        return lax.rem(spec + k, ns)

    def share_copy(lf, k):
        return pltpu.make_async_remote_copy(
            src_ref=own.at[pl.ds(lf * NDIR, NDIR), peer(k)],
            dst_ref=gathered.at[:, spec * nf + lf],
            send_sem=share_send.at[lf, k - 1], recv_sem=share_recv.at[lf, k - 1],
            device_id={"spec": peer(k)}, device_id_type=MESH,
        )

    def share_local(lf):
        return pltpu.make_async_copy(
            own.at[pl.ds(lf * NDIR, NDIR), spec], gathered.at[:, spec * nf + lf], share_own.at[lf]
        )

    def q_copy(k):
        return pltpu.make_async_remote_copy(
            src_ref=q_out.at[pl.ds(0, SOURCE_ITERS)], dst_ref=q_in.at[:, spec],
            send_sem=q_send.at[k - 1], recv_sem=q_recv.at[k - 1],
            device_id={"spec": peer(k)}, device_id_type=MESH,
        )

    swap = (tile > 0).astype(jnp.int32)

    def advance(group, carry):
        lf = group // 2
        way = lax.rem(group + swap, 2)
        ratio = jnp.float32(ratio_of[0])
        for k in range(1, nf):
            ratio = jnp.where(lf == k, ratio_of[k], ratio)
        speed = jnp.float32(0.65) / ratio
        start = lf * NDIR + way * half

        @pl.when(group == 2 * lf)
        def _():
            own_copy(lf).wait()

        for w in range(2):

            @pl.when((way == w) & comes[w])
            def _():
                halo_copy(lf, w, ways[w][1]).wait_recv()

        rim = row_of == (ROWS - 1) * (1 - way)
        place, turned = index_t[way, 6], index_t[way, 7]
        hmask = factor_t[way, 4]
        xs = [own[start + i] * mask for i in range(half)]
        hs = [take_rows(halo[start + i], place) * hmask for i in range(half)]
        coefs = []
        for i in range(half):
            ax = speed * jnp.float32(abs(math.cos(ANGLE[i])))
            ay = speed * jnp.float32(abs(math.sin(ANGLE[i])))
            coefs.append((ax, ay, one - ax - ay))
        for step in range(SUBSTEPS):
            for i in range(half):
                q = i // QUAD
                ax, ay, rest = coefs[i]
                lanes = index_t[way, 4 + q]
                x, h = xs[i], hs[i]
                side_x = take_lanes(take_rows(x, index_t[way, q]), lanes)
                side_y = take_lanes(jnp.where(rim, h, x), turned)
                xs[i] = (rest * x + (ax * factor_t[way, q]) * side_x + ay * side_y) * mask
                if step < SUBSTEPS - 1:
                    side_x = take_lanes(take_rows(h, index_t[way, 2 + q]), lanes)
                    side_y = take_lanes(h, turned)
                    hs[i] = (rest * h + (ax * factor_t[way, 2 + q]) * side_x + ay * side_y) * hmask
        for i in range(half):
            own[start + i] = xs[i]

        @pl.when(group == 2 * lf + 1)
        def _():
            for k in order:
                share_copy(lf, k).start()
            share_local(lf).start()

        return carry

    lax.fori_loop(0, 2 * nf, advance, 0)

    for lf in range(nf):
        share_local(lf).wait()
        for k in order:
            share_copy(lf, k).wait_recv()
    mask_row = mine(4)
    place8 = lax.broadcasted_iota(jnp.int32, (8, POINTS), 0)
    empty8 = jnp.zeros((8, POINTS), jnp.float32)
    freqs = [table_rows(place8, [1.1 ** (8 * b + s) for s in range(8)]) for b in range(blocks)]
    freq_root = [
        table_rows(place8, [math.sqrt(1.1 ** (8 * b + s)) for s in range(8)]) for b in range(blocks)
    ]
    freq_limit = [jnp.float32(0.08) / ratio for ratio in freqs]
    sums = [empty8] * blocks
    for d in range(NDIR):
        for b in range(blocks):
            sums[b] = sums[b] + gathered[d, 8 * b : 8 * b + 8, :]
    for step in range(SOURCE_ITERS):
        first = sum(ratio * t for ratio, t in zip(freqs, sums))
        second = sum(ratio * ratio * t for ratio, t in zip(freqs, sums))
        first = jnp.sum(first, axis=0, keepdims=True) * jnp.float32(1.0 / total_comps)
        second = jnp.sum(second, axis=0, keepdims=True) * jnp.float32(1.0 / total_comps)
        mean_ratio = (second + 0.1) / (first + 0.1)
        damping = jnp.float32(0.2 * 0.25) * first / (mean_ratio * mean_ratio)
        q_out[step : step + 1, :] = damping
        if step == SOURCE_ITERS - 1:
            break
        damping = jnp.broadcast_to(damping, (8, POINTS))
        damp = [damping * (ratio * ratio) for ratio in freqs]

        def relax(j, sums):
            sums = list(sums)
            for i in range(chunk):
                d = j * chunk + i
                g = grow_row[d]
                for b in range(blocks):
                    x = gathered[d, 8 * b : 8 * b + 8, :]
                    change = (g * freq_root[b] - damp[b]) * x
                    change = jnp.minimum(jnp.maximum(change, -freq_limit[b]), freq_limit[b])
                    x = jnp.maximum(x + change, 0.0) * mask_row
                    gathered[d, 8 * b : 8 * b + 8, :] = x
                    sums[b] = sums[b] + x
            return tuple(sums)

        sums = lax.fori_loop(0, NDIR // chunk, relax, (empty8,) * blocks)

    for k in order:
        q_copy(k).start()
    q_in[:, pl.ds(spec, 1), :] = q_out[0:SOURCE_ITERS, :].reshape(SOURCE_ITERS, 1, POINTS)
    root_spec = table_pick(spec, [math.sqrt(1.1 ** (nf * s)) for s in range(ns)])
    root = [root_spec * jnp.float32(math.sqrt(1.1**lf)) for lf in range(nf)]
    limit = [jnp.float32(0.08) / ratio for ratio in ratio_of]
    for lf in range(nf):
        for k in order:
            share_copy(lf, k).wait_send()
    for k in order:
        q_copy(k).wait_recv()
    dampings = [q_in[step] for step in range(SOURCE_ITERS)]
    damps = [[t * (ratio * ratio) for ratio in ratio_of] for t in dampings]

    def settle(j, carry):
        for i in range(chunk):
            d = j * chunk + i
            g = grow[d]
            for lf in range(nf):
                x = own[lf * NDIR + d]
                gain = g * root[lf]
                for step in range(SOURCE_ITERS):
                    change = (gain - damps[step][lf]) * x
                    change = jnp.minimum(jnp.maximum(change, -limit[lf]), limit[lf])
                    x = jnp.maximum(x + change, 0.0) * mask
                own[lf * NDIR + d] = x
        return carry

    lax.fori_loop(0, NDIR // chunk, settle, 0)

    for way, other, there in ways:

        @pl.when(there)
        def _():
            aux_copy(way, other).wait_send()
            halo_copy(nf - 1, way, other).wait_send()

    for k in order:
        q_copy(k).wait_send()


def body(nt, ns, spectra, wind_speed, wind_dir, sea_mask, neighbours):
    comps, tiles_dev, points = spectra.shape
    nf = comps // NDIR
    anywhere = pl.BlockSpec(memory_space=pl.ANY)
    dma = pltpu.SemaphoreType.DMA
    operands = [
        pltpu.with_memory_space_constraint(x, pltpu.HBM)
        for x in (spectra, wind_speed, wind_dir, sea_mask, neighbours.T)
    ]
    return pl.pallas_call(
        functools.partial(kernel, nt, ns, nf),
        out_shape=pltpu.VMEM(spectra.shape, jnp.float32),
        in_specs=[anywhere] * 5,
        out_specs=pl.BlockSpec(memory_space=pltpu.VMEM),
        scratch_shapes=[
            pltpu.VMEM((comps, tiles_dev, points), jnp.float32),
            pltpu.SMEM((4, tiles_dev), jnp.int32),
            pltpu.VMEM((6, tiles_dev, points), jnp.float32),
            pltpu.VMEM((tiles_dev, points), jnp.int32),
            pltpu.VMEM((2, 3, tiles_dev, points), jnp.int32),
            pltpu.VMEM((2, 3, tiles_dev, points), jnp.int32),
            pltpu.VMEM((NDIR, tiles_dev, points), jnp.float32),
            pltpu.VMEM((NDIR, 8, points), jnp.float32),
            pltpu.VMEM((NDIR, nf * ns, points), jnp.float32),
            pltpu.VMEM((8, points), jnp.float32),
            pltpu.VMEM((SOURCE_ITERS, tiles_dev, points), jnp.float32),
            pltpu.VMEM((2, 8, tiles_dev, points), jnp.int32),
            pltpu.VMEM((2, 5, tiles_dev, points), jnp.float32),
            dma((nf,)),
            dma((4,)),
            dma((2,)),
            dma((2,)),
            dma((nf, 2)),
            dma((nf, 2)),
            dma((nf, ns - 1)),
            dma((nf, ns - 1)),
            dma((nf,)),
            dma((ns - 1,)),
            dma((ns - 1,)),
        ],
        compiler_params=pltpu.CompilerParams(
            collective_id=0, has_side_effects=True, vmem_limit_bytes=16 * 1024 * 1024
        ),
    )(*operands)


def solution(mesh):
    placed = (
        P("spec", "tile", None),
        P("tile", None),
        P("tile", None),
        P("tile", None),
        P("tile", None),
    )
    return jax.shard_map(
        functools.partial(body, mesh.shape["tile"], mesh.shape["spec"]),
        mesh=mesh, in_specs=placed, out_specs=P("spec", "tile", None), check_vma=False,
    )
```

```python
import functools
import math

import jax
import jax.numpy as jnp
import numpy as np
from jax import lax
from jax.experimental import pallas as pl
from jax.experimental.pallas import tpu as pltpu
from jax.sharding import PartitionSpec as P

NDIR = 36
ROWS = 4
COLS = 32
SUBSTEPS = 4
SOURCE_ITERS = 3
QUAD = 9
POINTS = ROWS * COLS
MESH = pl.DeviceIdType.MESH

ANGLE = (np.arange(NDIR) + 0.5) * (2.0 * math.pi / NDIR)


def table_pick(index, values):
    out = jnp.float32(values[0])
    for k in range(1, len(values)):
        out = jnp.where(index == k, jnp.float32(values[k]), out)
    return out


def table_rows(row, values):
    out = jnp.full(row.shape, values[0], jnp.float32)
    for k in range(1, len(values)):
        out = jnp.where(row == k, jnp.float32(values[k]), out)
    return out


def take_rows(x, index):
    return jnp.take_along_axis(x, index, axis=0)


def take_lanes(x, index):
    return jnp.take_along_axis(x, index, axis=1)


def kernel(
    nt, ns, nf,
    spectra, speed_hbm, dir_hbm, mask_hbm, nb_hbm, own,
    halo, nb, small_f, small_i, aux_out, aux_in, grow, grow_row, gathered, q_out, q_in,
    index_t, factor_t,
    load_sem, small_sem, aux_send, aux_recv, halo_send, halo_recv,
    share_send, share_recv, share_own, q_send, q_recv, met,
):
    tile = lax.axis_index("tile")
    spec = lax.axis_index("spec")
    above, beneath = jnp.maximum(tile - 1, 0), jnp.minimum(tile + 1, nt - 1)
    tiles_dev = own.shape[1]
    comps = nf * NDIR
    total_comps = comps * ns
    blocks = nf * ns // 8
    half = NDIR // 2

    chips = ns // 2
    around = lax.rem(spec, 2) * chips + spec // 2

    def on_ring(offset):
        v = lax.rem(around + offset, ns)
        return lax.rem(v, chips) * 2 + v // chips

    greeted = [on_ring(offset) for offset in (1, ns - 1, chips)]
    barrier = pltpu.get_barrier_semaphore()
    ways = ((0, beneath, tile < nt - 1), (1, above, tile > 0))
    for way, other, there in ways:

        @pl.when(there)
        def _():
            pl.semaphore_signal(barrier, inc=1, device_id={"tile": other}, device_id_type=MESH)

    for other in greeted:
        pl.semaphore_signal(barrier, inc=1, device_id={"spec": other}, device_id_type=MESH)

    small = [
        pltpu.make_async_copy(nb_hbm, nb, small_sem.at[0]),
        pltpu.make_async_copy(mask_hbm, small_i, small_sem.at[1]),
        pltpu.make_async_copy(speed_hbm, small_f.at[0], small_sem.at[2]),
        pltpu.make_async_copy(dir_hbm, small_f.at[1], small_sem.at[3]),
    ]
    for copy in small:
        copy.start()

    def own_copy(lf):
        run = pl.ds(lf * NDIR, NDIR)
        return pltpu.make_async_copy(spectra.at[run], own.at[run], load_sem.at[lf])

    for lf in range(nf):
        own_copy(lf).start()

    def aux_copy(way, other):
        return pltpu.make_async_remote_copy(
            src_ref=aux_out.at[way], dst_ref=aux_in.at[way],
            send_sem=aux_send.at[way], recv_sem=aux_recv.at[way],
            device_id={"tile": other}, device_id_type=MESH,
        )

    def halo_copy(lf, way, other):
        run = pl.ds(lf * NDIR + way * half, half)
        return pltpu.make_async_remote_copy(
            src_ref=spectra.at[run], dst_ref=halo.at[run],
            send_sem=halo_send.at[lf, way], recv_sem=halo_recv.at[lf, way],
            device_id={"tile": other}, device_id_type=MESH,
        )

    pl.semaphore_wait(
        barrier, len(greeted) + (tile > 0).astype(jnp.int32) + (tile < nt - 1).astype(jnp.int32)
    )
    comes = (tile > 0, tile < nt - 1)
    for way, other, there in ways:

        @pl.when(there)
        def _():
            halo_copy(0, way, other).start()

    for other in greeted:
        pl.semaphore_signal(met, inc=1, device_id={"spec": other}, device_id_type=MESH)

    shape = (tiles_dev, POINTS)
    lane = lax.broadcasted_iota(jnp.int32, shape, 1)
    row_of = lane // COLS
    col_of = lane - row_of * COLS
    sublane = lax.broadcasted_iota(jnp.int32, shape, 0)
    small[0].wait()
    base = tile * tiles_dev

    def spread(k):
        wide = jnp.full(shape, nb[k, 0], jnp.int32)
        for s in range(1, tiles_dev):
            wide = jnp.where(sublane == s, nb[k, s], wide)
        return wide

    def local(wide, first):
        return jnp.clip(wide - first, 0, tiles_dev - 1)

    north_id, south_id, west_id, east_id = [spread(k) for k in range(4)]
    north_at, south_at = local(north_id, base - tiles_dev), local(south_id, base + tiles_dev)
    west_at, east_at = local(west_id, base), local(east_id, base)
    small[1].wait()
    mask_i = small_i[...]
    for way, place in ((0, south_at), (1, north_at)):
        aux_out[way, 0] = mask_i
        aux_out[way, 1] = jnp.where(west_id >= 0, take_rows(place, west_at), -1)
        aux_out[way, 2] = jnp.where(east_id >= 0, take_rows(place, east_at), -1)

    for way, other, there in ways:

        @pl.when(there)
        def _():
            aux_copy(way, other).start()

    for lf in range(1, nf):
        for way, other, there in ways:

            @pl.when(there)
            def _():
                halo_copy(lf, way, other).start()

    for way, other, there in ways:

        @pl.when(jnp.logical_not(comes[way]))
        def _():
            aux_in[way] = jnp.zeros(aux_in.shape[1:], jnp.int32)
            for lf in range(nf):
                run = pl.ds(lf * NDIR + way * half, half)
                halo[run] = jnp.zeros((half,) + shape, jnp.float32)

    small[2].wait()
    small[3].wait()
    scaled = small_f[0] * jnp.float32(0.2 * 0.03)
    small_f[2] = jnp.cos(small_f[1])
    small_f[3] = jnp.sin(small_f[1])
    small_f[4] = mask_i.astype(jnp.float32)
    small_f[5] = scaled

    def mine(k):
        return jnp.broadcast_to(small_f[k, pl.ds(spec, 1), :], (8, POINTS))

    for target, cos_w, sin_w, scale in (
        (grow, small_f[2], small_f[3], scaled), (grow_row, mine(2), mine(3), mine(5))
    ):
        along, across = scale * cos_w, scale * sin_w
        for d in range(QUAD):
            cos_d, sin_d = jnp.float32(math.cos(ANGLE[d])), jnp.float32(math.sin(ANGLE[d]))
            ahead = along * cos_d + across * sin_d
            aside = across * cos_d - along * sin_d
            target[d] = jnp.maximum(ahead, 0.0)
            target[QUAD + d] = jnp.maximum(aside, 0.0)
            target[2 * QUAD + d] = jnp.maximum(-ahead, 0.0)
            target[3 * QUAD + d] = jnp.maximum(-aside, 0.0)

    mask = mask_i.astype(jnp.float32)
    one = jnp.float32(1.0)
    zero = jnp.float32(0.0)
    empty = jnp.zeros(shape, jnp.float32)
    ratio_spec = table_pick(spec, [1.1 ** (nf * s) for s in range(ns)])
    ratio_of = [ratio_spec * jnp.float32(1.1**lf) for lf in range(nf)]

    def sideways(at, valid, edge):
        return (
            jnp.where(col_of == edge, at, sublane),
            jnp.where((col_of == COLS - 1 - edge) & jnp.logical_not(valid), zero, one),
        )

    lanes_of = (
        row_of * COLS + lax.rem(col_of + COLS - 1, COLS),
        row_of * COLS + lax.rem(col_of + 1, COLS),
    )
    side_own = (
        sideways(west_at, west_id >= 0, COLS - 1),
        sideways(east_at, east_id >= 0, 0),
    )
    for way, place, ident, turn in (
        (0, north_at, north_id, POINTS - COLS), (1, south_at, south_id, COLS)
    ):

        @pl.when(comes[way])
        def _():
            aux_copy(way, ways[way][1]).wait_recv()

        factor_t[way, 4] = jnp.where(ident >= 0, take_rows(aux_in[way, 0], place), 0).astype(
            jnp.float32
        )
        index_t[way, 6] = place
        index_t[way, 7] = lax.rem(lane + turn, POINTS)
        for q in range(2):
            side = way if q == 0 else 1 - way
            pull, keep = side_own[side]
            at = take_rows(aux_in[way, 1 + side], place)
            hpull, hkeep = sideways(jnp.maximum(at, 0), at >= 0, COLS - 1 if side == 0 else 0)
            index_t[way, q], index_t[way, 2 + q], index_t[way, 4 + q] = pull, hpull, lanes_of[side]
            factor_t[way, q], factor_t[way, 2 + q] = keep, hkeep

    chunk = NDIR // 6
    order = sorted(range(1, ns), key=lambda k: -min(k // 2, (ns - k) // 2))

    def peer(k):
        return lax.rem(spec + k, ns)

    def share_copy(lf, k):
        return pltpu.make_async_remote_copy(
            src_ref=own.at[pl.ds(lf * NDIR, NDIR), peer(k)],
            dst_ref=gathered.at[:, spec * nf + lf],
            send_sem=share_send.at[lf, k - 1], recv_sem=share_recv.at[lf, k - 1],
            device_id={"spec": peer(k)}, device_id_type=MESH,
        )

    def share_local(lf):
        return pltpu.make_async_copy(
            own.at[pl.ds(lf * NDIR, NDIR), spec], gathered.at[:, spec * nf + lf], share_own.at[lf]
        )

    def q_copy(k):
        return pltpu.make_async_remote_copy(
            src_ref=q_out.at[pl.ds(0, SOURCE_ITERS)], dst_ref=q_in.at[:, spec],
            send_sem=q_send.at[k - 1], recv_sem=q_recv.at[k - 1],
            device_id={"spec": peer(k)}, device_id_type=MESH,
        )

    swap = (tile > 0).astype(jnp.int32)

    def advance(group, carry):
        lf = group // 2
        way = lax.rem(group + swap, 2)
        ratio = jnp.float32(ratio_of[0])
        for k in range(1, nf):
            ratio = jnp.where(lf == k, ratio_of[k], ratio)
        speed = jnp.float32(0.65) / ratio
        start = lf * NDIR + way * half

        @pl.when(group == 2 * lf)
        def _():
            own_copy(lf).wait()

        for w in range(2):

            @pl.when((way == w) & comes[w])
            def _():
                halo_copy(lf, w, ways[w][1]).wait_recv()

        rim = row_of == (ROWS - 1) * (1 - way)
        place, turned = index_t[way, 6], index_t[way, 7]
        hmask = factor_t[way, 4]
        xs = [own[start + i] * mask for i in range(half)]
        hs = [take_rows(halo[start + i], place) * hmask for i in range(half)]
        coefs = []
        for i in range(half):
            ax = speed * jnp.float32(abs(math.cos(ANGLE[i])))
            ay = speed * jnp.float32(abs(math.sin(ANGLE[i])))
            coefs.append((ax, ay, one - ax - ay))
        for step in range(SUBSTEPS):
            for i in range(half):
                q = i // QUAD
                ax, ay, rest = coefs[i]
                lanes = index_t[way, 4 + q]
                x, h = xs[i], hs[i]
                side_x = take_lanes(take_rows(x, index_t[way, q]), lanes)
                side_y = take_lanes(jnp.where(rim, h, x), turned)
                xs[i] = (rest * x + (ax * factor_t[way, q]) * side_x + ay * side_y) * mask
                if step < SUBSTEPS - 1:
                    side_x = take_lanes(take_rows(h, index_t[way, 2 + q]), lanes)
                    side_y = take_lanes(h, turned)
                    hs[i] = (rest * h + (ax * factor_t[way, 2 + q]) * side_x + ay * side_y) * hmask
        for i in range(half):
            own[start + i] = xs[i]

        @pl.when(group == 1)
        def _():
            pl.semaphore_wait(met, len(greeted))

        @pl.when(group == 2 * lf + 1)
        def _():
            for k in order:
                share_copy(lf, k).start()
            share_local(lf).start()

        return carry

    lax.fori_loop(0, 2 * nf, advance, 0)

    def arrive(lf, carry):
        share_local(lf).wait()
        for k in order:
            share_copy(lf, k).wait_recv()
        return carry

    lax.fori_loop(0, nf, arrive, 0)
    mask_row = mine(4)
    place8 = lax.broadcasted_iota(jnp.int32, (8, POINTS), 0)
    empty8 = jnp.zeros((8, POINTS), jnp.float32)
    freqs = [table_rows(place8, [1.1 ** (8 * b + s) for s in range(8)]) for b in range(blocks)]
    freq_root = [
        table_rows(place8, [math.sqrt(1.1 ** (8 * b + s)) for s in range(8)]) for b in range(blocks)
    ]
    freq_limit = [jnp.float32(0.08) / ratio for ratio in freqs]

    def gather_sums(j, sums):
        sums = list(sums)
        for i in range(chunk):
            for b in range(blocks):
                sums[b] = sums[b] + gathered[j * chunk + i, 8 * b : 8 * b + 8, :]
        return tuple(sums)

    sums = lax.fori_loop(0, NDIR // chunk, gather_sums, (empty8,) * blocks)
    for step in range(SOURCE_ITERS):
        first = sum(ratio * t for ratio, t in zip(freqs, sums))
        second = sum(ratio * ratio * t for ratio, t in zip(freqs, sums))
        first = jnp.sum(first, axis=0, keepdims=True) * jnp.float32(1.0 / total_comps)
        second = jnp.sum(second, axis=0, keepdims=True) * jnp.float32(1.0 / total_comps)
        mean_ratio = (second + 0.1) / (first + 0.1)
        damping = jnp.float32(0.2 * 0.25) * first / (mean_ratio * mean_ratio)
        q_out[step : step + 1, :] = damping
        if step == SOURCE_ITERS - 1:
            break
        damping = jnp.broadcast_to(damping, (8, POINTS))
        damp = [damping * (ratio * ratio) for ratio in freqs]

        def relax(j, sums):
            sums = list(sums)
            for i in range(chunk):
                d = j * chunk + i
                g = grow_row[d]
                for b in range(blocks):
                    x = gathered[d, 8 * b : 8 * b + 8, :]
                    change = (g * freq_root[b] - damp[b]) * x
                    change = jnp.minimum(jnp.maximum(change, -freq_limit[b]), freq_limit[b])
                    x = jnp.maximum(x + change, 0.0) * mask_row
                    gathered[d, 8 * b : 8 * b + 8, :] = x
                    sums[b] = sums[b] + x
            return tuple(sums)

        sums = lax.fori_loop(0, NDIR // chunk, relax, (empty8,) * blocks)

    for k in order:
        q_copy(k).start()
    q_in[:, pl.ds(spec, 1), :] = q_out[0:SOURCE_ITERS, :].reshape(SOURCE_ITERS, 1, POINTS)
    root_spec = table_pick(spec, [math.sqrt(1.1 ** (nf * s)) for s in range(ns)])
    root = [root_spec * jnp.float32(math.sqrt(1.1**lf)) for lf in range(nf)]
    limit = [jnp.float32(0.08) / ratio for ratio in ratio_of]
    def left(lf, carry):
        for k in order:
            share_copy(lf, k).wait_send()
        return carry

    lax.fori_loop(0, nf, left, 0)
    for k in order:
        q_copy(k).wait_recv()
    dampings = [q_in[step] for step in range(SOURCE_ITERS)]
    damps = [[t * (ratio * ratio) for ratio in ratio_of] for t in dampings]

    def settle(j, carry):
        for i in range(chunk):
            d = j * chunk + i
            g = grow[d]
            for lf in range(nf):
                x = own[lf * NDIR + d]
                gain = g * root[lf]
                for step in range(SOURCE_ITERS):
                    change = (gain - damps[step][lf]) * x
                    change = jnp.minimum(jnp.maximum(change, -limit[lf]), limit[lf])
                    x = jnp.maximum(x + change, 0.0) * mask
                own[lf * NDIR + d] = x
        return carry

    lax.fori_loop(0, NDIR // chunk, settle, 0)

    for way, other, there in ways:

        @pl.when(there)
        def _():
            aux_copy(way, other).wait_send()
            for lf in range(nf):
                halo_copy(lf, way, other).wait_send()

    for k in order:
        q_copy(k).wait_send()


def body(nt, ns, spectra, wind_speed, wind_dir, sea_mask, neighbours):
    comps, tiles_dev, points = spectra.shape
    nf = comps // NDIR
    anywhere = pl.BlockSpec(memory_space=pl.ANY)
    dma = pltpu.SemaphoreType.DMA
    operands = [
        pltpu.with_memory_space_constraint(x, pltpu.HBM)
        for x in (spectra, wind_speed, wind_dir, sea_mask, neighbours.T)
    ]
    return pl.pallas_call(
        functools.partial(kernel, nt, ns, nf),
        out_shape=pltpu.VMEM(spectra.shape, jnp.float32),
        in_specs=[anywhere] * 5,
        out_specs=pl.BlockSpec(memory_space=pltpu.VMEM),
        scratch_shapes=[
            pltpu.VMEM((comps, tiles_dev, points), jnp.float32),
            pltpu.SMEM((4, tiles_dev), jnp.int32),
            pltpu.VMEM((6, tiles_dev, points), jnp.float32),
            pltpu.VMEM((tiles_dev, points), jnp.int32),
            pltpu.VMEM((2, 3, tiles_dev, points), jnp.int32),
            pltpu.VMEM((2, 3, tiles_dev, points), jnp.int32),
            pltpu.VMEM((NDIR, tiles_dev, points), jnp.float32),
            pltpu.VMEM((NDIR, 8, points), jnp.float32),
            pltpu.VMEM((NDIR, nf * ns, points), jnp.float32),
            pltpu.VMEM((8, points), jnp.float32),
            pltpu.VMEM((SOURCE_ITERS, tiles_dev, points), jnp.float32),
            pltpu.VMEM((2, 8, tiles_dev, points), jnp.int32),
            pltpu.VMEM((2, 5, tiles_dev, points), jnp.float32),
            dma((nf,)),
            dma((4,)),
            dma((2,)),
            dma((2,)),
            dma((nf, 2)),
            dma((nf, 2)),
            dma((nf, ns - 1)),
            dma((nf, ns - 1)),
            dma((nf,)),
            dma((ns - 1,)),
            dma((ns - 1,)),
            pltpu.SemaphoreType.REGULAR,
        ],
        compiler_params=pltpu.CompilerParams(
            collective_id=0, has_side_effects=True, vmem_limit_bytes=16 * 1024 * 1024
        ),
    )(*operands)


def solution(mesh):
    placed = (
        P("spec", "tile", None),
        P("tile", None),
        P("tile", None),
        P("tile", None),
        P("tile", None),
    )
    return jax.shard_map(
        functools.partial(body, mesh.shape["tile"], mesh.shape["spec"]),
        mesh=mesh, in_specs=placed, out_specs=P("spec", "tile", None), check_vma=False,
    )
```

```python
import functools
import math

import jax
import jax.numpy as jnp
import numpy as np
from jax import lax
from jax.experimental import pallas as pl
from jax.experimental.pallas import tpu as pltpu
from jax.sharding import PartitionSpec as P

NDIR = 36
ROWS = 4
COLS = 32
SUBSTEPS = 4
SOURCE_ITERS = 3
QUAD = 9
POINTS = ROWS * COLS
MESH = pl.DeviceIdType.MESH

ANGLE = (np.arange(NDIR) + 0.5) * (2.0 * math.pi / NDIR)


def table_pick(index, values):
    out = jnp.float32(values[0])
    for k in range(1, len(values)):
        out = jnp.where(index == k, jnp.float32(values[k]), out)
    return out


def table_rows(row, values):
    out = jnp.full(row.shape, values[0], jnp.float32)
    for k in range(1, len(values)):
        out = jnp.where(row == k, jnp.float32(values[k]), out)
    return out


def take_rows(x, index):
    return jnp.take_along_axis(x, index, axis=0)


def take_lanes(x, index):
    return jnp.take_along_axis(x, index, axis=1)


def kernel(
    nt, ns, nf,
    spectra, speed_hbm, dir_hbm, mask_hbm, nb_hbm, own,
    halo, nb, small_f, small_i, aux_out, aux_in, grow, grow_row, gathered, q_out, q_in,
    index_t, factor_t,
    load_sem, small_sem, aux_send, aux_recv, halo_send, halo_recv,
    share_send, share_recv, share_own, q_send, q_recv, met,
):
    tile = lax.axis_index("tile")
    spec = lax.axis_index("spec")
    above, beneath = jnp.maximum(tile - 1, 0), jnp.minimum(tile + 1, nt - 1)
    tiles_dev = own.shape[1]
    comps = nf * NDIR
    total_comps = comps * ns
    blocks = nf
    half = NDIR // 2

    chips = ns // 2
    around = lax.rem(spec, 2) * chips + spec // 2

    def on_ring(offset):
        v = lax.rem(around + offset, ns)
        return lax.rem(v, chips) * 2 + v // chips

    greeted = [on_ring(offset) for offset in (1, ns - 1, chips)]
    barrier = pltpu.get_barrier_semaphore()
    ways = ((0, beneath, tile < nt - 1), (1, above, tile > 0))
    for way, other, there in ways:

        @pl.when(there)
        def _():
            pl.semaphore_signal(barrier, inc=1, device_id={"tile": other}, device_id_type=MESH)

    for other in greeted:
        pl.semaphore_signal(barrier, inc=1, device_id={"spec": other}, device_id_type=MESH)

    small = [
        pltpu.make_async_copy(nb_hbm, nb, small_sem.at[0]),
        pltpu.make_async_copy(mask_hbm, small_i, small_sem.at[1]),
        pltpu.make_async_copy(speed_hbm, small_f.at[0], small_sem.at[2]),
        pltpu.make_async_copy(dir_hbm, small_f.at[1], small_sem.at[3]),
    ]
    for copy in small:
        copy.start()

    def own_copy(lf):
        run = pl.ds(lf * NDIR, NDIR)
        return pltpu.make_async_copy(spectra.at[run], own.at[run], load_sem.at[lf])

    for lf in range(nf):
        own_copy(lf).start()

    def aux_copy(way, other):
        return pltpu.make_async_remote_copy(
            src_ref=aux_out.at[way], dst_ref=aux_in.at[way],
            send_sem=aux_send.at[way], recv_sem=aux_recv.at[way],
            device_id={"tile": other}, device_id_type=MESH,
        )

    def halo_copy(lf, way, other):
        run = pl.ds(lf * NDIR + way * half, half)
        return pltpu.make_async_remote_copy(
            src_ref=spectra.at[run], dst_ref=halo.at[run],
            send_sem=halo_send.at[way], recv_sem=halo_recv.at[lf, way],
            device_id={"tile": other}, device_id_type=MESH,
        )

    pl.semaphore_wait(
        barrier, len(greeted) + (tile > 0).astype(jnp.int32) + (tile < nt - 1).astype(jnp.int32)
    )
    comes = (tile > 0, tile < nt - 1)
    for way, other, there in ways:

        @pl.when(there)
        def _():
            halo_copy(0, way, other).start()

    for other in greeted:
        pl.semaphore_signal(met, inc=1, device_id={"spec": other}, device_id_type=MESH)

    shape = (tiles_dev, POINTS)
    lane = lax.broadcasted_iota(jnp.int32, shape, 1)
    row_of = lane // COLS
    col_of = lane - row_of * COLS
    sublane = lax.broadcasted_iota(jnp.int32, shape, 0)
    small[0].wait()
    base = tile * tiles_dev

    def spread(k):
        wide = jnp.full(shape, nb[k, 0], jnp.int32)
        for s in range(1, tiles_dev):
            wide = jnp.where(sublane == s, nb[k, s], wide)
        return wide

    def local(wide, first):
        return jnp.clip(wide - first, 0, tiles_dev - 1)

    north_id, south_id, west_id, east_id = [spread(k) for k in range(4)]
    north_at, south_at = local(north_id, base - tiles_dev), local(south_id, base + tiles_dev)
    west_at, east_at = local(west_id, base), local(east_id, base)
    small[1].wait()
    mask_i = small_i[...]
    for way, place in ((0, south_at), (1, north_at)):
        aux_out[way, 0] = mask_i
        aux_out[way, 1] = jnp.where(west_id >= 0, take_rows(place, west_at), -1)
        aux_out[way, 2] = jnp.where(east_id >= 0, take_rows(place, east_at), -1)

    for way, other, there in ways:

        @pl.when(there)
        def _():
            aux_copy(way, other).start()

    for lf in range(1, nf):
        for way, other, there in ways:

            @pl.when(there)
            def _():
                halo_copy(lf, way, other).start()

    for way, other, there in ways:

        @pl.when(jnp.logical_not(comes[way]))
        def _():
            aux_in[way] = jnp.zeros(aux_in.shape[1:], jnp.int32)
            for lf in range(nf):
                run = pl.ds(lf * NDIR + way * half, half)
                halo[run] = jnp.zeros((half,) + shape, jnp.float32)

    small[2].wait()
    small[3].wait()
    scaled = small_f[0] * jnp.float32(0.2 * 0.03)
    small_f[2] = jnp.cos(small_f[1])
    small_f[3] = jnp.sin(small_f[1])
    small_f[4] = mask_i.astype(jnp.float32)
    small_f[5] = scaled

    def mine(k):
        return jnp.broadcast_to(small_f[k, pl.ds(spec, 1), :], (8, POINTS))

    for target, cos_w, sin_w, scale in (
        (grow, small_f[2], small_f[3], scaled), (grow_row, mine(2), mine(3), mine(5))
    ):
        along, across = scale * cos_w, scale * sin_w
        for d in range(QUAD):
            cos_d, sin_d = jnp.float32(math.cos(ANGLE[d])), jnp.float32(math.sin(ANGLE[d]))
            ahead = along * cos_d + across * sin_d
            aside = across * cos_d - along * sin_d
            target[d] = jnp.maximum(ahead, 0.0)
            target[QUAD + d] = jnp.maximum(aside, 0.0)
            target[2 * QUAD + d] = jnp.maximum(-ahead, 0.0)
            target[3 * QUAD + d] = jnp.maximum(-aside, 0.0)

    mask = mask_i.astype(jnp.float32)
    one = jnp.float32(1.0)
    zero = jnp.float32(0.0)
    empty = jnp.zeros(shape, jnp.float32)
    ratio_spec = table_pick(spec, [1.1 ** (nf * s) for s in range(ns)])
    ratio_of = [ratio_spec * jnp.float32(1.1**lf) for lf in range(nf)]

    def sideways(at, valid, edge):
        return (
            jnp.where(col_of == edge, at, sublane),
            jnp.where((col_of == COLS - 1 - edge) & jnp.logical_not(valid), zero, one),
        )

    lanes_of = (
        row_of * COLS + lax.rem(col_of + COLS - 1, COLS),
        row_of * COLS + lax.rem(col_of + 1, COLS),
    )
    side_own = (
        sideways(west_at, west_id >= 0, COLS - 1),
        sideways(east_at, east_id >= 0, 0),
    )
    def halo_tables(way):
        place, ident, turn = (
            (north_at, north_id, POINTS - COLS), (south_at, south_id, COLS)
        )[way]

        @pl.when(comes[way])
        def _():
            aux_copy(way, ways[way][1]).wait_recv()

        factor_t[way, 4] = jnp.where(ident >= 0, take_rows(aux_in[way, 0], place), 0).astype(
            jnp.float32
        )
        index_t[way, 6] = place
        index_t[way, 7] = lax.rem(lane + turn, POINTS)
        for q in range(2):
            side = way if q == 0 else 1 - way
            pull, keep = side_own[side]
            at = take_rows(aux_in[way, 1 + side], place)
            hpull, hkeep = sideways(jnp.maximum(at, 0), at >= 0, COLS - 1 if side == 0 else 0)
            index_t[way, q], index_t[way, 2 + q], index_t[way, 4 + q] = pull, hpull, lanes_of[side]
            factor_t[way, q], factor_t[way, 2 + q] = keep, hkeep

    chunk = NDIR // 6
    order = sorted(range(1, ns), key=lambda k: -min(k // 2, (ns - k) // 2))

    def peer(k):
        return lax.rem(spec + k, ns)

    def share_copy(lf, k):
        return pltpu.make_async_remote_copy(
            src_ref=own.at[pl.ds(lf * NDIR, NDIR), peer(k)],
            dst_ref=gathered.at[:, lf * ns + spec],
            send_sem=share_send.at[lf], recv_sem=share_recv.at[lf],
            device_id={"spec": peer(k)}, device_id_type=MESH,
        )

    def share_local(lf):
        return pltpu.make_async_copy(
            own.at[pl.ds(lf * NDIR, NDIR), spec], gathered.at[:, lf * ns + spec], share_own.at[lf]
        )

    def share_all(sem):
        return pltpu.make_async_copy(
            gathered.at[:, pl.ds(0, ns - 1)], gathered.at[:, pl.ds(ns, ns - 1)], sem
        )

    def q_all(sem):
        return pltpu.make_async_copy(
            q_in.at[:, pl.ds(0, ns - 1)], q_in.at[:, pl.ds(0, ns - 1)], sem
        )

    def q_copy(k):
        return pltpu.make_async_remote_copy(
            src_ref=q_out.at[pl.ds(0, SOURCE_ITERS)], dst_ref=q_in.at[:, spec],
            send_sem=q_send.at[0], recv_sem=q_recv.at[0],
            device_id={"spec": peer(k)}, device_id_type=MESH,
        )

    swap = (tile > 0).astype(jnp.int32)
    edge = (tile == 0) | (tile == nt - 1)
    swap_edge = (tile == nt - 1).astype(jnp.int32)

    def advance(group, carry):
        lf = jnp.where(edge, lax.rem(group, nf), group // 2)
        way = jnp.where(edge, lax.rem(group // nf + swap_edge, 2), lax.rem(group + swap, 2))
        opens = jnp.where(edge, group < nf, lax.rem(group, 2) == 0)
        ratio = jnp.float32(ratio_of[0])
        for k in range(1, nf):
            ratio = jnp.where(lf == k, ratio_of[k], ratio)
        speed = jnp.float32(0.65) / ratio
        start = lf * NDIR + way * half

        @pl.when(opens)
        def _():
            own_copy(lf).wait()

        for w in range(2):

            @pl.when((way == w) & (lf == 0))
            def _():
                halo_tables(w)

            @pl.when((way == w) & comes[w])
            def _():
                halo_copy(lf, w, ways[w][1]).wait_recv()

        rim = row_of == (ROWS - 1) * (1 - way)
        place, turned = index_t[way, 6], index_t[way, 7]
        hmask = factor_t[way, 4]
        xs = [own[start + i] * mask for i in range(half)]
        hs = [take_rows(halo[start + i], place) * hmask for i in range(half)]
        coefs = []
        for i in range(half):
            ax = speed * jnp.float32(abs(math.cos(ANGLE[i])))
            ay = speed * jnp.float32(abs(math.sin(ANGLE[i])))
            coefs.append((ax, ay, one - ax - ay))
        for step in range(SUBSTEPS):
            for i in range(half):
                q = i // QUAD
                ax, ay, rest = coefs[i]
                lanes = index_t[way, 4 + q]
                x, h = xs[i], hs[i]
                side_x = take_lanes(take_rows(x, index_t[way, q]), lanes)
                side_y = take_lanes(jnp.where(rim, h, x), turned)
                xs[i] = (rest * x + (ax * factor_t[way, q]) * side_x + ay * side_y) * mask
                if step < SUBSTEPS - 1:
                    side_x = take_lanes(take_rows(h, index_t[way, 2 + q]), lanes)
                    side_y = take_lanes(h, turned)
                    hs[i] = (rest * h + (ax * factor_t[way, 2 + q]) * side_x + ay * side_y) * hmask
        for i in range(half):
            own[start + i] = xs[i]

        @pl.when(jnp.logical_not(opens) & (lf == 0))
        def _():
            pl.semaphore_wait(met, len(greeted))

        @pl.when(jnp.logical_not(opens))
        def _():
            for k in order:
                share_copy(lf, k).start()
            share_local(lf).start()

        return carry

    lax.fori_loop(0, 2 * nf, advance, 0)

    mask_row = mine(4)
    place8 = lax.broadcasted_iota(jnp.int32, (8, POINTS), 0)
    empty8 = jnp.zeros((8, POINTS), jnp.float32)
    freqs = [table_rows(place8, [1.1 ** (nf * s + b) for s in range(ns)]) for b in range(blocks)]
    freq_root = [
        table_rows(place8, [math.sqrt(1.1 ** (nf * s + b)) for s in range(ns)]) for b in range(blocks)
    ]
    freq_limit = [jnp.float32(0.08) / ratio for ratio in freqs]

    sums = []
    for b in range(blocks):
        share_local(b).wait()
        share_all(share_recv.at[b]).wait()
        parts = [empty8] * 4
        for d in range(NDIR):
            parts[d % 4] = parts[d % 4] + gathered[d, 8 * b : 8 * b + 8, :]
        sums.append((parts[0] + parts[1]) + (parts[2] + parts[3]))
    for step in range(SOURCE_ITERS):
        first = sum(ratio * t for ratio, t in zip(freqs, sums))
        second = sum(ratio * ratio * t for ratio, t in zip(freqs, sums))
        first = jnp.sum(first, axis=0, keepdims=True) * jnp.float32(1.0 / total_comps)
        second = jnp.sum(second, axis=0, keepdims=True) * jnp.float32(1.0 / total_comps)
        mean_ratio = (second + 0.1) / (first + 0.1)
        damping = jnp.float32(0.2 * 0.25) * first / (mean_ratio * mean_ratio)
        q_out[step : step + 1, :] = damping
        if step == SOURCE_ITERS - 1:
            break
        damping = jnp.broadcast_to(damping, (8, POINTS))
        damp = [damping * (ratio * ratio) for ratio in freqs]

        def relax(j, sums):
            sums = list(sums)
            for i in range(chunk):
                d = j * chunk + i
                g = grow_row[d]
                for b in range(blocks):
                    x = gathered[d, 8 * b : 8 * b + 8, :]
                    change = (g * freq_root[b] - damp[b]) * x
                    change = jnp.minimum(jnp.maximum(change, -freq_limit[b]), freq_limit[b])
                    x = jnp.maximum(x + change, 0.0) * mask_row
                    gathered[d, 8 * b : 8 * b + 8, :] = x
                    sums[b] = sums[b] + x
            return tuple(sums)

        sums = lax.fori_loop(0, NDIR // chunk, relax, (empty8,) * blocks)

    for k in order:
        q_copy(k).start()
    q_in[:, pl.ds(spec, 1), :] = q_out[0:SOURCE_ITERS, :].reshape(SOURCE_ITERS, 1, POINTS)
    root_spec = table_pick(spec, [math.sqrt(1.1 ** (nf * s)) for s in range(ns)])
    root = [root_spec * jnp.float32(math.sqrt(1.1**lf)) for lf in range(nf)]
    limit = [jnp.float32(0.08) / ratio for ratio in ratio_of]
    for lf in range(nf):
        share_all(share_send.at[lf]).wait()
    q_all(q_recv.at[0]).wait()
    dampings = [q_in[step] for step in range(SOURCE_ITERS)]
    damps = [[t * (ratio * ratio) for ratio in ratio_of] for t in dampings]

    def settle(j, carry):
        for i in range(chunk):
            d = j * chunk + i
            g = grow[d]
            for lf in range(nf):
                x = own[lf * NDIR + d]
                gain = g * root[lf]
                for step in range(SOURCE_ITERS):
                    change = (gain - damps[step][lf]) * x
                    change = jnp.minimum(jnp.maximum(change, -limit[lf]), limit[lf])
                    x = jnp.maximum(x + change, 0.0) * mask
                own[lf * NDIR + d] = x
        return carry

    lax.fori_loop(0, NDIR // chunk, settle, 0)

    for way, other, there in ways:

        @pl.when(there)
        def _():
            aux_copy(way, other).wait_send()
            pltpu.make_async_copy(
                halo.at[pl.ds(0, nf * half)], halo.at[pl.ds(nf * half, nf * half)], halo_send.at[way]
            ).wait()

    q_all(q_send.at[0]).wait()


def body(nt, ns, spectra, wind_speed, wind_dir, sea_mask, neighbours):
    comps, tiles_dev, points = spectra.shape
    nf = comps // NDIR
    anywhere = pl.BlockSpec(memory_space=pl.ANY)
    dma = pltpu.SemaphoreType.DMA
    operands = [
        pltpu.with_memory_space_constraint(x, pltpu.HBM)
        for x in (spectra, wind_speed, wind_dir, sea_mask, neighbours.T)
    ]
    return pl.pallas_call(
        functools.partial(kernel, nt, ns, nf),
        out_shape=pltpu.VMEM(spectra.shape, jnp.float32),
        in_specs=[anywhere] * 5,
        out_specs=pl.BlockSpec(memory_space=pltpu.VMEM),
        scratch_shapes=[
            pltpu.VMEM((comps, tiles_dev, points), jnp.float32),
            pltpu.SMEM((4, tiles_dev), jnp.int32),
            pltpu.VMEM((6, tiles_dev, points), jnp.float32),
            pltpu.VMEM((tiles_dev, points), jnp.int32),
            pltpu.VMEM((2, 3, tiles_dev, points), jnp.int32),
            pltpu.VMEM((2, 3, tiles_dev, points), jnp.int32),
            pltpu.VMEM((NDIR, tiles_dev, points), jnp.float32),
            pltpu.VMEM((NDIR, 8, points), jnp.float32),
            pltpu.VMEM((NDIR, nf * ns, points), jnp.float32),
            pltpu.VMEM((8, points), jnp.float32),
            pltpu.VMEM((SOURCE_ITERS, tiles_dev, points), jnp.float32),
            pltpu.VMEM((2, 8, tiles_dev, points), jnp.int32),
            pltpu.VMEM((2, 5, tiles_dev, points), jnp.float32),
            dma((nf,)),
            dma((4,)),
            dma((2,)),
            dma((2,)),
            dma((2,)),
            dma((nf, 2)),
            dma((nf,)),
            dma((nf,)),
            dma((nf,)),
            dma((1,)),
            dma((1,)),
            pltpu.SemaphoreType.REGULAR,
        ],
        compiler_params=pltpu.CompilerParams(
            collective_id=0, has_side_effects=True, vmem_limit_bytes=16 * 1024 * 1024
        ),
    )(*operands)


def solution(mesh):
    placed = (
        P("spec", "tile", None),
        P("tile", None),
        P("tile", None),
        P("tile", None),
        P("tile", None),
    )
    return jax.shard_map(
        functools.partial(body, mesh.shape["tile"], mesh.shape["spec"]),
        mesh=mesh, in_specs=placed, out_specs=P("spec", "tile", None), check_vma=False,
    )
```

```python
import functools
import math

import jax
import jax.numpy as jnp
import numpy as np
from jax import lax
from jax.experimental import pallas as pl
from jax.experimental.pallas import tpu as pltpu
from jax.sharding import PartitionSpec as P

NDIR = 36
ROWS = 4
COLS = 32
SUBSTEPS = 4
SOURCE_ITERS = 3
QUAD = 9
POINTS = ROWS * COLS
MESH = pl.DeviceIdType.MESH

ANGLE = (np.arange(NDIR) + 0.5) * (2.0 * math.pi / NDIR)


def table_pick(index, values):
    out = jnp.float32(values[0])
    for k in range(1, len(values)):
        out = jnp.where(index == k, jnp.float32(values[k]), out)
    return out


def table_rows(row, values):
    out = jnp.full(row.shape, values[0], jnp.float32)
    for k in range(1, len(values)):
        out = jnp.where(row == k, jnp.float32(values[k]), out)
    return out


def take_rows(x, index):
    return jnp.take_along_axis(x, index, axis=0)


def take_lanes(x, index):
    return jnp.take_along_axis(x, index, axis=1)


def kernel(
    nt, ns, nf,
    spectra, speed_hbm, dir_hbm, mask_hbm, nb_hbm, own,
    halo, nb, small_f, small_i, aux_out, aux_in, grow, grow_row, gathered, q_out, q_in,
    index_t, factor_t,
    load_sem, small_sem, aux_send, aux_recv, halo_send, halo_recv,
    share_send, share_recv, share_own, q_send, q_recv, met,
):
    tile = lax.axis_index("tile")
    spec = lax.axis_index("spec")
    above, beneath = jnp.maximum(tile - 1, 0), jnp.minimum(tile + 1, nt - 1)
    tiles_dev = own.shape[1]
    comps = nf * NDIR
    total_comps = comps * ns
    blocks = nf
    half = NDIR // 2

    def ring_place(s):
        return s // 4 * 4 + lax.rem(s, 2) * 2 + lax.rem(s // 2, 2)

    around = ring_place(spec)
    greeted = [ring_place(lax.rem(around + step, ns)) for step in (ns // 2, 1, ns - 1)]
    barrier = pltpu.get_barrier_semaphore()
    ways = ((0, beneath, tile < nt - 1), (1, above, tile > 0))
    for way, other, there in ways:

        @pl.when(there)
        def _():
            pl.semaphore_signal(barrier, inc=1, device_id={"tile": other}, device_id_type=MESH)

    for other in greeted:
        pl.semaphore_signal(barrier, inc=1, device_id={"spec": other}, device_id_type=MESH)

    small = [
        pltpu.make_async_copy(nb_hbm, nb, small_sem.at[0]),
        pltpu.make_async_copy(mask_hbm, small_i, small_sem.at[1]),
        pltpu.make_async_copy(speed_hbm, small_f.at[0], small_sem.at[2]),
        pltpu.make_async_copy(dir_hbm, small_f.at[1], small_sem.at[3]),
    ]
    for copy in small:
        copy.start()

    def own_copy(lf):
        run = pl.ds(lf * NDIR, NDIR)
        return pltpu.make_async_copy(spectra.at[run], own.at[run], load_sem.at[lf])

    for lf in range(nf):
        own_copy(lf).start()

    def aux_copy(way, other):
        return pltpu.make_async_remote_copy(
            src_ref=aux_out.at[way], dst_ref=aux_in.at[way],
            send_sem=aux_send.at[way], recv_sem=aux_recv.at[way],
            device_id={"tile": other}, device_id_type=MESH,
        )

    def halo_copy(lf, way, other):
        run = pl.ds(lf * NDIR + way * half, half)
        return pltpu.make_async_remote_copy(
            src_ref=spectra.at[run], dst_ref=halo.at[run],
            send_sem=halo_send.at[way], recv_sem=halo_recv.at[lf, way],
            device_id={"tile": other}, device_id_type=MESH,
        )

    pl.semaphore_wait(
        barrier, len(greeted) + (tile > 0).astype(jnp.int32) + (tile < nt - 1).astype(jnp.int32)
    )
    comes = (tile > 0, tile < nt - 1)
    for way, other, there in ways:

        @pl.when(there)
        def _():
            halo_copy(0, way, other).start()

    for other in greeted:
        pl.semaphore_signal(met, inc=1, device_id={"spec": other}, device_id_type=MESH)

    shape = (tiles_dev, POINTS)
    lane = lax.broadcasted_iota(jnp.int32, shape, 1)
    row_of = lane // COLS
    col_of = lane - row_of * COLS
    sublane = lax.broadcasted_iota(jnp.int32, shape, 0)
    small[0].wait()
    base = tile * tiles_dev

    def spread(k):
        wide = jnp.full(shape, nb[k, 0], jnp.int32)
        for s in range(1, tiles_dev):
            wide = jnp.where(sublane == s, nb[k, s], wide)
        return wide

    def local(wide, first):
        return jnp.clip(wide - first, 0, tiles_dev - 1)

    north_id, south_id, west_id, east_id = [spread(k) for k in range(4)]
    north_at, south_at = local(north_id, base - tiles_dev), local(south_id, base + tiles_dev)
    west_at, east_at = local(west_id, base), local(east_id, base)
    small[1].wait()
    mask_i = small_i[...]
    for way, place in ((0, south_at), (1, north_at)):
        aux_out[way, 0] = mask_i
        aux_out[way, 1] = jnp.where(west_id >= 0, take_rows(place, west_at), -1)
        aux_out[way, 2] = jnp.where(east_id >= 0, take_rows(place, east_at), -1)

    for way, other, there in ways:

        @pl.when(there)
        def _():
            aux_copy(way, other).start()

    for lf in range(1, nf):
        for way, other, there in ways:

            @pl.when(there)
            def _():
                halo_copy(lf, way, other).start()

    for way, other, there in ways:

        @pl.when(jnp.logical_not(comes[way]))
        def _():
            aux_in[way] = jnp.zeros(aux_in.shape[1:], jnp.int32)
            for lf in range(nf):
                run = pl.ds(lf * NDIR + way * half, half)
                halo[run] = jnp.zeros((half,) + shape, jnp.float32)

    mask = mask_i.astype(jnp.float32)
    one = jnp.float32(1.0)
    zero = jnp.float32(0.0)
    empty = jnp.zeros(shape, jnp.float32)
    ratio_spec = table_pick(spec, [1.1 ** (nf * s) for s in range(ns)])
    ratio_of = [ratio_spec * jnp.float32(1.1**lf) for lf in range(nf)]

    def sideways(at, valid, edge):
        return (
            jnp.where(col_of == edge, at, sublane),
            jnp.where((col_of == COLS - 1 - edge) & jnp.logical_not(valid), zero, one),
        )

    lanes_of = (
        row_of * COLS + lax.rem(col_of + COLS - 1, COLS),
        row_of * COLS + lax.rem(col_of + 1, COLS),
    )
    side_own = (
        sideways(west_at, west_id >= 0, COLS - 1),
        sideways(east_at, east_id >= 0, 0),
    )
    def halo_tables(way):
        place, ident, turn = (
            (north_at, north_id, POINTS - COLS), (south_at, south_id, COLS)
        )[way]

        @pl.when(comes[way])
        def _():
            aux_copy(way, ways[way][1]).wait_recv()

        factor_t[way, 4] = jnp.where(ident >= 0, take_rows(aux_in[way, 0], place), 0).astype(
            jnp.float32
        )
        index_t[way, 6] = place
        index_t[way, 7] = lax.rem(lane + turn, POINTS)
        for q in range(2):
            side = way if q == 0 else 1 - way
            pull, keep = side_own[side]
            at = take_rows(aux_in[way, 1 + side], place)
            hpull, hkeep = sideways(jnp.maximum(at, 0), at >= 0, COLS - 1 if side == 0 else 0)
            index_t[way, q], index_t[way, 2 + q], index_t[way, 4 + q] = pull, hpull, lanes_of[side]
            factor_t[way, q], factor_t[way, 2 + q] = keep, hkeep

    chunk = NDIR // 6
    order = sorted(range(1, ns), key=lambda k: -min(k // 2, (ns - k) // 2))

    def peer(k):
        return lax.rem(spec + k, ns)

    def share_copy(lf, k, d=0, count=NDIR):
        return pltpu.make_async_remote_copy(
            src_ref=own.at[pl.ds(lf * NDIR + d, count), peer(k)],
            dst_ref=gathered.at[pl.ds(d, count), lf * ns + spec],
            send_sem=share_send.at[lf], recv_sem=share_recv.at[lf],
            device_id={"spec": peer(k)}, device_id_type=MESH,
        )

    def share_local(lf):
        return pltpu.make_async_copy(
            own.at[pl.ds(lf * NDIR, NDIR), spec], gathered.at[:, lf * ns + spec], share_own.at[lf]
        )

    def share_all(sem):
        return pltpu.make_async_copy(
            gathered.at[:, pl.ds(0, ns - 1)], gathered.at[:, pl.ds(ns, ns - 1)], sem
        )

    def q_all(sem):
        return pltpu.make_async_copy(
            q_in.at[:, pl.ds(0, ns - 1)], q_in.at[:, pl.ds(0, ns - 1)], sem
        )

    def q_copy(k):
        return pltpu.make_async_remote_copy(
            src_ref=q_out.at[pl.ds(0, SOURCE_ITERS)], dst_ref=q_in.at[:, spec],
            send_sem=q_send.at[0], recv_sem=q_recv.at[0],
            device_id={"spec": peer(k)}, device_id_type=MESH,
        )

    swap = (tile > 0).astype(jnp.int32)
    edge = (tile <= 1) | (tile == nt - 1)

    def advance(group, carry):
        lf = jnp.where(edge, lax.rem(group, nf), group // 2)
        way = jnp.where(edge, lax.rem(group // nf + swap, 2), lax.rem(group + swap, 2))
        opens = jnp.where(edge, group < nf, lax.rem(group, 2) == 0)
        ratio = jnp.float32(ratio_of[0])
        for k in range(1, nf):
            ratio = jnp.where(lf == k, ratio_of[k], ratio)
        speed = jnp.float32(0.65) / ratio
        start = lf * NDIR + way * half

        @pl.when(opens)
        def _():
            own_copy(lf).wait()

        for w in range(2):

            @pl.when((way == w) & (lf == 0))
            def _():
                halo_tables(w)

            @pl.when((way == w) & comes[w])
            def _():
                halo_copy(lf, w, ways[w][1]).wait_recv()

        rim = row_of == (ROWS - 1) * (1 - way)
        place, turned = index_t[way, 6], index_t[way, 7]
        hmask = factor_t[way, 4]
        xs = [own[start + i] * mask for i in range(half)]
        hs = [take_rows(halo[start + i], place) * hmask for i in range(half)]
        coefs = []
        for i in range(half):
            ax = speed * jnp.float32(abs(math.cos(ANGLE[i])))
            ay = speed * jnp.float32(abs(math.sin(ANGLE[i])))
            coefs.append((ax, ay, one - ax - ay))
        for step in range(SUBSTEPS):
            for i in range(half):
                q = i // QUAD
                ax, ay, rest = coefs[i]
                lanes = index_t[way, 4 + q]
                x, h = xs[i], hs[i]
                side_x = take_lanes(take_rows(x, index_t[way, q]), lanes)
                side_y = take_lanes(jnp.where(rim, h, x), turned)
                xs[i] = (rest * x + (ax * factor_t[way, q]) * side_x + ay * side_y) * mask
                if step < SUBSTEPS - 1:
                    side_x = take_lanes(take_rows(h, index_t[way, 2 + q]), lanes)
                    side_y = take_lanes(h, turned)
                    hs[i] = (rest * h + (ax * factor_t[way, 2 + q]) * side_x + ay * side_y) * hmask
        for i in range(half):
            own[start + i] = xs[i]

        @pl.when(group == jnp.where(edge, 0, 1))
        def _():
            pl.semaphore_wait(met, len(greeted))

        @pl.when(edge)
        def _():
            for k in order:
                share_copy(lf, k, way * half, half).start()

        @pl.when(jnp.logical_not(edge | opens))
        def _():
            for k in order:
                share_copy(lf, k).start()

        @pl.when(jnp.logical_not(opens))
        def _():
            share_local(lf).start()

        return carry

    lax.fori_loop(0, 2 * nf, advance, 0)

    small[2].wait()
    small[3].wait()
    scaled = small_f[0] * jnp.float32(0.2 * 0.03)
    small_f[2] = jnp.cos(small_f[1])
    small_f[3] = jnp.sin(small_f[1])
    small_f[4] = mask_i.astype(jnp.float32)
    small_f[5] = scaled

    def mine(k):
        return jnp.broadcast_to(small_f[k, pl.ds(spec, 1), :], (8, POINTS))

    for target, cos_w, sin_w, scale in (
        (grow, small_f[2], small_f[3], scaled), (grow_row, mine(2), mine(3), mine(5))
    ):
        along, across = scale * cos_w, scale * sin_w
        for d in range(QUAD):
            cos_d, sin_d = jnp.float32(math.cos(ANGLE[d])), jnp.float32(math.sin(ANGLE[d]))
            ahead = along * cos_d + across * sin_d
            aside = across * cos_d - along * sin_d
            target[d] = jnp.maximum(ahead, 0.0)
            target[QUAD + d] = jnp.maximum(aside, 0.0)
            target[2 * QUAD + d] = jnp.maximum(-ahead, 0.0)
            target[3 * QUAD + d] = jnp.maximum(-aside, 0.0)

    mask_row = mine(4)
    place8 = lax.broadcasted_iota(jnp.int32, (8, POINTS), 0)
    empty8 = jnp.zeros((8, POINTS), jnp.float32)
    freqs = [table_rows(place8, [1.1 ** (nf * s + b) for s in range(ns)]) for b in range(blocks)]
    freq_root = [
        table_rows(place8, [math.sqrt(1.1 ** (nf * s + b)) for s in range(ns)]) for b in range(blocks)
    ]
    freq_limit = [jnp.float32(0.08) / ratio for ratio in freqs]

    sums = []
    for b in range(blocks):
        share_local(b).wait()
        share_all(share_recv.at[b]).wait()
        parts = [empty8] * 4
        for d in range(NDIR):
            parts[d % 4] = parts[d % 4] + gathered[d, 8 * b : 8 * b + 8, :]
        sums.append((parts[0] + parts[1]) + (parts[2] + parts[3]))
    for step in range(SOURCE_ITERS):
        first = sum(ratio * t for ratio, t in zip(freqs, sums))
        second = sum(ratio * ratio * t for ratio, t in zip(freqs, sums))
        first = jnp.sum(first, axis=0, keepdims=True) * jnp.float32(1.0 / total_comps)
        second = jnp.sum(second, axis=0, keepdims=True) * jnp.float32(1.0 / total_comps)
        mean_ratio = (second + 0.1) / (first + 0.1)
        damping = jnp.float32(0.2 * 0.25) * first / (mean_ratio * mean_ratio)
        q_out[step : step + 1, :] = damping
        if step == SOURCE_ITERS - 1:
            break
        damping = jnp.broadcast_to(damping, (8, POINTS))
        damp = [damping * (ratio * ratio) for ratio in freqs]

        def relax(j, sums):
            sums = list(sums)
            for i in range(chunk):
                d = j * chunk + i
                g = grow_row[d]
                for b in range(blocks):
                    x = gathered[d, 8 * b : 8 * b + 8, :]
                    change = (g * freq_root[b] - damp[b]) * x
                    change = jnp.minimum(jnp.maximum(change, -freq_limit[b]), freq_limit[b])
                    x = jnp.maximum(x + change, 0.0) * mask_row
                    gathered[d, 8 * b : 8 * b + 8, :] = x
                    sums[b] = sums[b] + x
            return tuple(sums)

        sums = lax.fori_loop(0, NDIR // chunk, relax, (empty8,) * blocks)

    for k in order:
        q_copy(k).start()
    q_in[:, pl.ds(spec, 1), :] = q_out[0:SOURCE_ITERS, :].reshape(SOURCE_ITERS, 1, POINTS)
    root_spec = table_pick(spec, [math.sqrt(1.1 ** (nf * s)) for s in range(ns)])
    root = [root_spec * jnp.float32(math.sqrt(1.1**lf)) for lf in range(nf)]
    limit = [jnp.float32(0.08) / ratio for ratio in ratio_of]
    for lf in range(nf):
        share_all(share_send.at[lf]).wait()
    q_all(q_recv.at[0]).wait()
    dampings = [q_in[step] for step in range(SOURCE_ITERS)]
    damps = [[t * (ratio * ratio) for ratio in ratio_of] for t in dampings]

    def settle(j, carry):
        for i in range(chunk):
            d = j * chunk + i
            g = grow[d]
            for lf in range(nf):
                x = own[lf * NDIR + d]
                gain = g * root[lf]
                for step in range(SOURCE_ITERS):
                    change = (gain - damps[step][lf]) * x
                    change = jnp.minimum(jnp.maximum(change, -limit[lf]), limit[lf])
                    x = jnp.maximum(x + change, 0.0) * mask
                own[lf * NDIR + d] = x
        return carry

    lax.fori_loop(0, NDIR // chunk, settle, 0)

    for way, other, there in ways:

        @pl.when(there)
        def _():
            aux_copy(way, other).wait_send()
            pltpu.make_async_copy(
                halo.at[pl.ds(0, nf * half)], halo.at[pl.ds(nf * half, nf * half)], halo_send.at[way]
            ).wait()

    q_all(q_send.at[0]).wait()


def body(nt, ns, spectra, wind_speed, wind_dir, sea_mask, neighbours):
    comps, tiles_dev, points = spectra.shape
    nf = comps // NDIR
    anywhere = pl.BlockSpec(memory_space=pl.ANY)
    dma = pltpu.SemaphoreType.DMA
    operands = [
        pltpu.with_memory_space_constraint(x, pltpu.HBM)
        for x in (spectra, wind_speed, wind_dir, sea_mask, neighbours.T)
    ]
    return pl.pallas_call(
        functools.partial(kernel, nt, ns, nf),
        out_shape=pltpu.VMEM(spectra.shape, jnp.float32),
        in_specs=[anywhere] * 5,
        out_specs=pl.BlockSpec(memory_space=pltpu.VMEM),
        scratch_shapes=[
            pltpu.VMEM((comps, tiles_dev, points), jnp.float32),
            pltpu.SMEM((4, tiles_dev), jnp.int32),
            pltpu.VMEM((6, tiles_dev, points), jnp.float32),
            pltpu.VMEM((tiles_dev, points), jnp.int32),
            pltpu.VMEM((2, 3, tiles_dev, points), jnp.int32),
            pltpu.VMEM((2, 3, tiles_dev, points), jnp.int32),
            pltpu.VMEM((NDIR, tiles_dev, points), jnp.float32),
            pltpu.VMEM((NDIR, 8, points), jnp.float32),
            pltpu.VMEM((NDIR, nf * ns, points), jnp.float32),
            pltpu.VMEM((8, points), jnp.float32),
            pltpu.VMEM((SOURCE_ITERS, tiles_dev, points), jnp.float32),
            pltpu.VMEM((2, 8, tiles_dev, points), jnp.int32),
            pltpu.VMEM((2, 5, tiles_dev, points), jnp.float32),
            dma((nf,)),
            dma((4,)),
            dma((2,)),
            dma((2,)),
            dma((2,)),
            dma((nf, 2)),
            dma((nf,)),
            dma((nf,)),
            dma((nf,)),
            dma((1,)),
            dma((1,)),
            pltpu.SemaphoreType.REGULAR,
        ],
        compiler_params=pltpu.CompilerParams(
            collective_id=0, has_side_effects=True, vmem_limit_bytes=16 * 1024 * 1024
        ),
    )(*operands)


def solution(mesh):
    placed = (
        P("spec", "tile", None),
        P("tile", None),
        P("tile", None),
        P("tile", None),
        P("tile", None),
    )
    return jax.shard_map(
        functools.partial(body, mesh.shape["tile"], mesh.shape["spec"]),
        mesh=mesh, in_specs=placed, out_specs=P("spec", "tile", None), check_vma=False,
    )
```

```python
import functools
import math

import jax
import jax.numpy as jnp
import numpy as np
from jax import lax
from jax.experimental import pallas as pl
from jax.experimental.pallas import tpu as pltpu
from jax.sharding import PartitionSpec as P

NDIR = 36
ROWS = 4
COLS = 32
SUBSTEPS = 4
SOURCE_ITERS = 3
QUAD = 9
POINTS = ROWS * COLS
MESH = pl.DeviceIdType.MESH

ANGLE = (np.arange(NDIR) + 0.5) * (2.0 * math.pi / NDIR)


def table_pick(index, values):
    out = jnp.float32(values[0])
    for k in range(1, len(values)):
        out = jnp.where(index == k, jnp.float32(values[k]), out)
    return out


def table_rows(row, values):
    out = jnp.full(row.shape, values[0], jnp.float32)
    for k in range(1, len(values)):
        out = jnp.where(row == k, jnp.float32(values[k]), out)
    return out


def take_rows(x, index):
    return jnp.take_along_axis(x, index, axis=0)


def take_lanes(x, index):
    return jnp.take_along_axis(x, index, axis=1)


def kernel(
    nt, ns, nf,
    spectra, speed_hbm, dir_hbm, mask_hbm, nb_hbm, own,
    halo, nb, small_f, small_i, aux_out, aux_in, grow, grow_row, gathered, q_out, q_in,
    index_t, factor_t,
    load_sem, small_sem, aux_send, aux_recv, halo_send, halo_recv,
    share_send, share_recv, share_own, q_send, q_recv, met,
):
    tile = lax.axis_index("tile")
    spec = lax.axis_index("spec")
    above, beneath = jnp.maximum(tile - 1, 0), jnp.minimum(tile + 1, nt - 1)
    tiles_dev = own.shape[1]
    comps = nf * NDIR
    total_comps = comps * ns
    blocks = nf
    half = NDIR // 2

    def ring_place(s):
        return s // 4 * 4 + lax.rem(s, 2) * 2 + lax.rem(s // 2, 2)

    around = ring_place(spec)
    greeted = [ring_place(lax.rem(around + step, ns)) for step in (ns // 2, 1, ns - 1)]
    barrier = pltpu.get_barrier_semaphore()
    ways = ((0, beneath, tile < nt - 1), (1, above, tile > 0))
    for way, other, there in ways:

        @pl.when(there)
        def _():
            pl.semaphore_signal(barrier, inc=1, device_id={"tile": other}, device_id_type=MESH)

    for other in greeted:
        pl.semaphore_signal(barrier, inc=1, device_id={"spec": other}, device_id_type=MESH)

    small = [
        pltpu.make_async_copy(nb_hbm, nb, small_sem.at[0]),
        pltpu.make_async_copy(mask_hbm, small_i, small_sem.at[1]),
        pltpu.make_async_copy(speed_hbm, small_f.at[0], small_sem.at[2]),
        pltpu.make_async_copy(dir_hbm, small_f.at[1], small_sem.at[3]),
    ]
    for copy in small:
        copy.start()

    def own_copy(lf):
        run = pl.ds(lf * NDIR, NDIR)
        return pltpu.make_async_copy(spectra.at[run], own.at[run], load_sem.at[lf])

    for lf in range(nf):
        own_copy(lf).start()

    def aux_copy(way, other):
        return pltpu.make_async_remote_copy(
            src_ref=aux_out.at[way], dst_ref=aux_in.at[way],
            send_sem=aux_send.at[way], recv_sem=aux_recv.at[way],
            device_id={"tile": other}, device_id_type=MESH,
        )

    def halo_copy(lf, way, other):
        run = pl.ds(lf * NDIR + way * half, half)
        return pltpu.make_async_remote_copy(
            src_ref=spectra.at[run], dst_ref=halo.at[run],
            send_sem=halo_send.at[way], recv_sem=halo_recv.at[lf, way],
            device_id={"tile": other}, device_id_type=MESH,
        )

    comes = (tile > 0, tile < nt - 1)

    def start_halos(lf):
        for way, other, there in ways[::-1]:

            @pl.when(there)
            def _():
                halo_copy(lf, way, other).start()

    pl.semaphore_wait(
        barrier, len(greeted) + (tile > 0).astype(jnp.int32) + (tile < nt - 1).astype(jnp.int32)
    )
    @pl.when(tile == 0)
    def _():
        start_halos(0)

    for other in greeted:
        pl.semaphore_signal(met, inc=1, device_id={"spec": other}, device_id_type=MESH)

    shape = (tiles_dev, POINTS)
    lane = lax.broadcasted_iota(jnp.int32, shape, 1)
    row_of = lane // COLS
    col_of = lane - row_of * COLS
    sublane = lax.broadcasted_iota(jnp.int32, shape, 0)
    small[0].wait()
    base = tile * tiles_dev

    def spread(k):
        wide = jnp.full(shape, nb[k, 0], jnp.int32)
        for s in range(1, tiles_dev):
            wide = jnp.where(sublane == s, nb[k, s], wide)
        return wide

    def local(wide, first):
        return jnp.clip(wide - first, 0, tiles_dev - 1)

    north_id, south_id, west_id, east_id = [spread(k) for k in range(4)]
    north_at, south_at = local(north_id, base - tiles_dev), local(south_id, base + tiles_dev)
    west_at, east_at = local(west_id, base), local(east_id, base)
    small[1].wait()
    mask_i = small_i[...]
    for way, place in ((0, south_at), (1, north_at)):
        aux_out[way, 0] = mask_i
        aux_out[way, 1] = jnp.where(west_id >= 0, take_rows(place, west_at), -1)
        aux_out[way, 2] = jnp.where(east_id >= 0, take_rows(place, east_at), -1)

    for way, other, there in ways[::-1]:

        @pl.when(there)
        def _():
            aux_copy(way, other).start()

    @pl.when(tile > 0)
    def _():
        start_halos(0)

    for lf in range(1, nf):
        start_halos(lf)

    for way, other, there in ways:

        @pl.when(jnp.logical_not(comes[way]))
        def _():
            aux_in[way] = jnp.zeros(aux_in.shape[1:], jnp.int32)
            for lf in range(nf):
                run = pl.ds(lf * NDIR + way * half, half)
                halo[run] = jnp.zeros((half,) + shape, jnp.float32)

    mask = mask_i.astype(jnp.float32)
    one = jnp.float32(1.0)
    zero = jnp.float32(0.0)
    empty = jnp.zeros(shape, jnp.float32)
    ratio_spec = table_pick(spec, [1.1 ** (nf * s) for s in range(ns)])
    ratio_of = [ratio_spec * jnp.float32(1.1**lf) for lf in range(nf)]

    def sideways(at, valid, edge):
        return (
            jnp.where(col_of == edge, at, sublane),
            jnp.where((col_of == COLS - 1 - edge) & jnp.logical_not(valid), zero, one),
        )

    lanes_of = (
        row_of * COLS + lax.rem(col_of + COLS - 1, COLS),
        row_of * COLS + lax.rem(col_of + 1, COLS),
    )
    side_own = (
        sideways(west_at, west_id >= 0, COLS - 1),
        sideways(east_at, east_id >= 0, 0),
    )
    def halo_tables(way):
        place, ident, turn = (
            (north_at, north_id, POINTS - COLS), (south_at, south_id, COLS)
        )[way]

        @pl.when(comes[way])
        def _():
            aux_copy(way, ways[way][1]).wait_recv()

        factor_t[way, 4] = jnp.where(ident >= 0, take_rows(aux_in[way, 0], place), 0).astype(
            jnp.float32
        )
        index_t[way, 6] = place
        index_t[way, 7] = lax.rem(lane + turn, POINTS)
        for q in range(2):
            side = way if q == 0 else 1 - way
            pull, keep = side_own[side]
            at = take_rows(aux_in[way, 1 + side], place)
            hpull, hkeep = sideways(jnp.maximum(at, 0), at >= 0, COLS - 1 if side == 0 else 0)
            index_t[way, q], index_t[way, 2 + q], index_t[way, 4 + q] = pull, hpull, lanes_of[side]
            factor_t[way, q], factor_t[way, 2 + q] = keep, hkeep

    chunk = NDIR // 6
    order = sorted(range(1, ns), key=lambda k: -min(k // 2, (ns - k) // 2))

    def peer(k):
        return lax.rem(spec + k, ns)

    def share_copy(lf, k, d=0, count=NDIR):
        return pltpu.make_async_remote_copy(
            src_ref=own.at[pl.ds(lf * NDIR + d, count), peer(k)],
            dst_ref=gathered.at[pl.ds(d, count), lf * ns + spec],
            send_sem=share_send.at[lf], recv_sem=share_recv.at[lf],
            device_id={"spec": peer(k)}, device_id_type=MESH,
        )

    def share_local(lf):
        return pltpu.make_async_copy(
            own.at[pl.ds(lf * NDIR, NDIR), spec], gathered.at[:, lf * ns + spec], share_own.at[lf]
        )

    def share_all(sem):
        return pltpu.make_async_copy(
            gathered.at[:, pl.ds(0, ns - 1)], gathered.at[:, pl.ds(ns, ns - 1)], sem
        )

    def q_all(sem):
        return pltpu.make_async_copy(
            q_in.at[:, pl.ds(0, ns - 1)], q_in.at[:, pl.ds(0, ns - 1)], sem
        )

    def q_copy(k):
        return pltpu.make_async_remote_copy(
            src_ref=q_out.at[pl.ds(0, SOURCE_ITERS)], dst_ref=q_in.at[:, spec],
            send_sem=q_send.at[0], recv_sem=q_recv.at[0],
            device_id={"spec": peer(k)}, device_id_type=MESH,
        )

    swap = (tile > 0).astype(jnp.int32)
    edge = (tile <= 1) | (tile == nt - 1)

    def advance(group, carry):
        lf = jnp.where(edge, lax.rem(group, nf), group // 2)
        way = jnp.where(edge, lax.rem(group // nf + swap, 2), lax.rem(group + swap, 2))
        opens = jnp.where(edge, group < nf, lax.rem(group, 2) == 0)
        ratio = jnp.float32(ratio_of[0])
        for k in range(1, nf):
            ratio = jnp.where(lf == k, ratio_of[k], ratio)
        speed = jnp.float32(0.65) / ratio
        start = lf * NDIR + way * half

        @pl.when(opens)
        def _():
            own_copy(lf).wait()

        for w in range(2):

            @pl.when((way == w) & (lf == 0))
            def _():
                halo_tables(w)

            @pl.when((way == w) & comes[w])
            def _():
                halo_copy(lf, w, ways[w][1]).wait_recv()

        rim = row_of == (ROWS - 1) * (1 - way)
        place, turned = index_t[way, 6], index_t[way, 7]
        hmask = factor_t[way, 4]
        xs = [own[start + i] * mask for i in range(half)]
        hs = [take_rows(halo[start + i], place) * hmask for i in range(half)]
        coefs = []
        for i in range(half):
            ax = speed * jnp.float32(abs(math.cos(ANGLE[i])))
            ay = speed * jnp.float32(abs(math.sin(ANGLE[i])))
            coefs.append((ax, ay, one - ax - ay))
        for step in range(SUBSTEPS):
            for i in range(half):
                q = i // QUAD
                ax, ay, rest = coefs[i]
                lanes = index_t[way, 4 + q]
                x, h = xs[i], hs[i]
                side_x = take_lanes(take_rows(x, index_t[way, q]), lanes)
                side_y = take_lanes(jnp.where(rim, h, x), turned)
                xs[i] = (rest * x + (ax * factor_t[way, q]) * side_x + ay * side_y) * mask
                if step < SUBSTEPS - 1:
                    side_x = take_lanes(take_rows(h, index_t[way, 2 + q]), lanes)
                    side_y = take_lanes(h, turned)
                    hs[i] = (rest * h + (ax * factor_t[way, 2 + q]) * side_x + ay * side_y) * hmask
        for i in range(half):
            own[start + i] = xs[i]

        @pl.when(group == jnp.where(edge, 0, 1))
        def _():
            pl.semaphore_wait(met, len(greeted))

        @pl.when(edge)
        def _():
            for k in order:
                share_copy(lf, k, way * half, half).start()

        @pl.when(jnp.logical_not(edge | opens))
        def _():
            for k in order:
                share_copy(lf, k).start()

        @pl.when(jnp.logical_not(opens))
        def _():
            share_local(lf).start()

        return carry

    lax.fori_loop(0, 2 * nf, advance, 0)

    small[2].wait()
    small[3].wait()
    scaled = small_f[0] * jnp.float32(0.2 * 0.03)
    small_f[2] = jnp.cos(small_f[1])
    small_f[3] = jnp.sin(small_f[1])
    small_f[4] = mask_i.astype(jnp.float32)
    small_f[5] = scaled

    def mine(k):
        return jnp.broadcast_to(small_f[k, pl.ds(spec, 1), :], (8, POINTS))

    for target, cos_w, sin_w, scale in (
        (grow, small_f[2], small_f[3], scaled), (grow_row, mine(2), mine(3), mine(5))
    ):
        along, across = scale * cos_w, scale * sin_w
        for d in range(QUAD):
            cos_d, sin_d = jnp.float32(math.cos(ANGLE[d])), jnp.float32(math.sin(ANGLE[d]))
            ahead = along * cos_d + across * sin_d
            aside = across * cos_d - along * sin_d
            target[d] = jnp.maximum(ahead, 0.0)
            target[QUAD + d] = jnp.maximum(aside, 0.0)
            target[2 * QUAD + d] = jnp.maximum(-ahead, 0.0)
            target[3 * QUAD + d] = jnp.maximum(-aside, 0.0)

    mask_row = mine(4)
    place8 = lax.broadcasted_iota(jnp.int32, (8, POINTS), 0)
    empty8 = jnp.zeros((8, POINTS), jnp.float32)
    freqs = [table_rows(place8, [1.1 ** (nf * s + b) for s in range(ns)]) for b in range(blocks)]
    freq_root = [
        table_rows(place8, [math.sqrt(1.1 ** (nf * s + b)) for s in range(ns)]) for b in range(blocks)
    ]
    freq_limit = [jnp.float32(0.08) / ratio for ratio in freqs]

    sums = []
    for b in range(blocks):
        share_local(b).wait()
        share_all(share_recv.at[b]).wait()
        parts = [empty8] * 4
        for d in range(NDIR):
            parts[d % 4] = parts[d % 4] + gathered[d, 8 * b : 8 * b + 8, :]
        sums.append((parts[0] + parts[1]) + (parts[2] + parts[3]))
    for step in range(SOURCE_ITERS):
        first = sum(ratio * t for ratio, t in zip(freqs, sums))
        second = sum(ratio * ratio * t for ratio, t in zip(freqs, sums))
        first = jnp.sum(first, axis=0, keepdims=True) * jnp.float32(1.0 / total_comps)
        second = jnp.sum(second, axis=0, keepdims=True) * jnp.float32(1.0 / total_comps)
        mean_ratio = (second + 0.1) / (first + 0.1)
        damping = jnp.float32(0.2 * 0.25) * first / (mean_ratio * mean_ratio)
        q_out[step : step + 1, :] = damping
        if step == SOURCE_ITERS - 1:
            break
        damping = jnp.broadcast_to(damping, (8, POINTS))
        damp = [damping * (ratio * ratio) for ratio in freqs]

        def relax(j, sums):
            sums = list(sums)
            for i in range(chunk):
                d = j * chunk + i
                g = grow_row[d]
                for b in range(blocks):
                    x = gathered[d, 8 * b : 8 * b + 8, :]
                    change = (g * freq_root[b] - damp[b]) * x
                    change = jnp.minimum(jnp.maximum(change, -freq_limit[b]), freq_limit[b])
                    x = jnp.maximum(x + change, 0.0) * mask_row
                    gathered[d, 8 * b : 8 * b + 8, :] = x
                    sums[b] = sums[b] + x
            return tuple(sums)

        sums = lax.fori_loop(0, NDIR // chunk, relax, (empty8,) * blocks)

    for k in order:
        q_copy(k).start()
    q_in[:, pl.ds(spec, 1), :] = q_out[0:SOURCE_ITERS, :].reshape(SOURCE_ITERS, 1, POINTS)
    root_spec = table_pick(spec, [math.sqrt(1.1 ** (nf * s)) for s in range(ns)])
    root = [root_spec * jnp.float32(math.sqrt(1.1**lf)) for lf in range(nf)]
    limit = [jnp.float32(0.08) / ratio for ratio in ratio_of]
    for lf in range(nf):
        share_all(share_send.at[lf]).wait()
    q_all(q_recv.at[0]).wait()
    dampings = [q_in[step] for step in range(SOURCE_ITERS)]
    damps = [[t * (ratio * ratio) for ratio in ratio_of] for t in dampings]

    def settle(j, carry):
        for i in range(chunk):
            d = j * chunk + i
            g = grow[d]
            for lf in range(nf):
                x = own[lf * NDIR + d]
                gain = g * root[lf]
                for step in range(SOURCE_ITERS):
                    change = (gain - damps[step][lf]) * x
                    change = jnp.minimum(jnp.maximum(change, -limit[lf]), limit[lf])
                    x = jnp.maximum(x + change, 0.0) * mask
                own[lf * NDIR + d] = x
        return carry

    lax.fori_loop(0, NDIR // chunk, settle, 0)

    for way, other, there in ways:

        @pl.when(there)
        def _():
            aux_copy(way, other).wait_send()
            pltpu.make_async_copy(
                halo.at[pl.ds(0, nf * half)], halo.at[pl.ds(nf * half, nf * half)], halo_send.at[way]
            ).wait()

    q_all(q_send.at[0]).wait()


def body(nt, ns, spectra, wind_speed, wind_dir, sea_mask, neighbours):
    comps, tiles_dev, points = spectra.shape
    nf = comps // NDIR
    anywhere = pl.BlockSpec(memory_space=pl.ANY)
    dma = pltpu.SemaphoreType.DMA
    operands = [
        pltpu.with_memory_space_constraint(x, pltpu.HBM)
        for x in (spectra, wind_speed, wind_dir, sea_mask, neighbours.T)
    ]
    return pl.pallas_call(
        functools.partial(kernel, nt, ns, nf),
        out_shape=pltpu.VMEM(spectra.shape, jnp.float32),
        in_specs=[anywhere] * 5,
        out_specs=pl.BlockSpec(memory_space=pltpu.VMEM),
        scratch_shapes=[
            pltpu.VMEM((comps, tiles_dev, points), jnp.float32),
            pltpu.SMEM((4, tiles_dev), jnp.int32),
            pltpu.VMEM((6, tiles_dev, points), jnp.float32),
            pltpu.VMEM((tiles_dev, points), jnp.int32),
            pltpu.VMEM((2, 3, tiles_dev, points), jnp.int32),
            pltpu.VMEM((2, 3, tiles_dev, points), jnp.int32),
            pltpu.VMEM((NDIR, tiles_dev, points), jnp.float32),
            pltpu.VMEM((NDIR, 8, points), jnp.float32),
            pltpu.VMEM((NDIR, nf * ns, points), jnp.float32),
            pltpu.VMEM((8, points), jnp.float32),
            pltpu.VMEM((SOURCE_ITERS, tiles_dev, points), jnp.float32),
            pltpu.VMEM((2, 8, tiles_dev, points), jnp.int32),
            pltpu.VMEM((2, 5, tiles_dev, points), jnp.float32),
            dma((nf,)),
            dma((4,)),
            dma((2,)),
            dma((2,)),
            dma((2,)),
            dma((nf, 2)),
            dma((nf,)),
            dma((nf,)),
            dma((nf,)),
            dma((1,)),
            dma((1,)),
            pltpu.SemaphoreType.REGULAR,
        ],
        compiler_params=pltpu.CompilerParams(
            collective_id=0, has_side_effects=True, vmem_limit_bytes=16 * 1024 * 1024
        ),
    )(*operands)


def solution(mesh):
    placed = (
        P("spec", "tile", None),
        P("tile", None),
        P("tile", None),
        P("tile", None),
        P("tile", None),
    )
    return jax.shard_map(
        functools.partial(body, mesh.shape["tile"], mesh.shape["spec"]),
        mesh=mesh, in_specs=placed, out_specs=P("spec", "tile", None), check_vma=False,
    )
```

```python
import functools
import math

import jax
import jax.numpy as jnp
import numpy as np
from jax import lax
from jax.experimental import pallas as pl
from jax.experimental.pallas import tpu as pltpu
from jax.sharding import PartitionSpec as P

NDIR = 36
ROWS = 4
COLS = 32
SUBSTEPS = 4
SOURCE_ITERS = 3
QUAD = 9
POINTS = ROWS * COLS
MESH = pl.DeviceIdType.MESH

ANGLE = (np.arange(NDIR) + 0.5) * (2.0 * math.pi / NDIR)


def table_pick(index, values):
    out = jnp.float32(values[0])
    for k in range(1, len(values)):
        out = jnp.where(index == k, jnp.float32(values[k]), out)
    return out


def table_rows(row, values):
    out = jnp.full(row.shape, values[0], jnp.float32)
    for k in range(1, len(values)):
        out = jnp.where(row == k, jnp.float32(values[k]), out)
    return out


def take_rows(x, index):
    return jnp.take_along_axis(x, index, axis=0)


def take_lanes(x, index):
    return jnp.take_along_axis(x, index, axis=1)


def kernel(
    nt, ns, nf,
    spectra, speed_hbm, dir_hbm, mask_hbm, nb_hbm, own,
    halo, nb, small_f, small_i, aux_out, aux_in, grow, grow_row, gathered, q_out, q_in,
    index_t, factor_t,
    load_sem, small_sem, aux_send, aux_recv, halo_send, halo_recv,
    share_send, share_recv, share_own, q_send, q_recv, met,
):
    tile = lax.axis_index("tile")
    spec = lax.axis_index("spec")
    above, beneath = jnp.maximum(tile - 1, 0), jnp.minimum(tile + 1, nt - 1)
    tiles_dev = own.shape[1]
    comps = nf * NDIR
    total_comps = comps * ns
    blocks = nf
    half = NDIR // 2

    def ring_place(s):
        return s // 4 * 4 + lax.rem(s, 2) * 2 + lax.rem(s // 2, 2)

    around = ring_place(spec)
    greeted = [ring_place(lax.rem(around + step, ns)) for step in (ns // 2, 1, ns - 1)]
    barrier = pltpu.get_barrier_semaphore()
    ways = ((0, beneath, tile < nt - 1), (1, above, tile > 0))
    for way, other, there in ways:

        @pl.when(there)
        def _():
            pl.semaphore_signal(barrier, inc=1, device_id={"tile": other}, device_id_type=MESH)

    for other in greeted:
        pl.semaphore_signal(barrier, inc=1, device_id={"spec": other}, device_id_type=MESH)

    small = [
        pltpu.make_async_copy(nb_hbm, nb, small_sem.at[0]),
        pltpu.make_async_copy(mask_hbm, small_i, small_sem.at[1]),
        pltpu.make_async_copy(speed_hbm, small_f.at[0], small_sem.at[2]),
        pltpu.make_async_copy(dir_hbm, small_f.at[1], small_sem.at[3]),
    ]
    for copy in small:
        copy.start()

    def own_copy(lf):
        run = pl.ds(lf * NDIR, NDIR)
        return pltpu.make_async_copy(spectra.at[run], own.at[run], load_sem.at[lf])

    for lf in range(nf):
        own_copy(lf).start()

    def aux_copy(way, other):
        return pltpu.make_async_remote_copy(
            src_ref=aux_out.at[way], dst_ref=aux_in.at[way],
            send_sem=aux_send.at[way], recv_sem=aux_recv.at[way],
            device_id={"tile": other}, device_id_type=MESH,
        )

    def halo_copy(lf, way, other):
        run = pl.ds(lf * NDIR + way * half, half)
        return pltpu.make_async_remote_copy(
            src_ref=spectra.at[run], dst_ref=halo.at[run],
            send_sem=halo_send.at[way], recv_sem=halo_recv.at[lf, way],
            device_id={"tile": other}, device_id_type=MESH,
        )

    comes = (tile > 0, tile < nt - 1)

    def start_halos(lf):
        for way, other, there in ways[::-1]:

            @pl.when(there)
            def _():
                halo_copy(lf, way, other).start()

    pl.semaphore_wait(
        barrier, len(greeted) + (tile > 0).astype(jnp.int32) + (tile < nt - 1).astype(jnp.int32)
    )
    @pl.when(tile == 0)
    def _():
        start_halos(0)

    for other in greeted:
        pl.semaphore_signal(met, inc=1, device_id={"spec": other}, device_id_type=MESH)

    shape = (tiles_dev, POINTS)
    lane = lax.broadcasted_iota(jnp.int32, shape, 1)
    row_of = lane // COLS
    col_of = lane - row_of * COLS
    sublane = lax.broadcasted_iota(jnp.int32, shape, 0)
    small[0].wait()
    base = tile * tiles_dev

    def spread(k):
        wide = jnp.full(shape, nb[k, 0], jnp.int32)
        for s in range(1, tiles_dev):
            wide = jnp.where(sublane == s, nb[k, s], wide)
        return wide

    def local(wide, first):
        return jnp.clip(wide - first, 0, tiles_dev - 1)

    north_id, south_id, west_id, east_id = [spread(k) for k in range(4)]
    north_at, south_at = local(north_id, base - tiles_dev), local(south_id, base + tiles_dev)
    west_at, east_at = local(west_id, base), local(east_id, base)
    small[1].wait()
    mask_i = small_i[...]
    for way, place in ((0, south_at), (1, north_at)):
        aux_out[way, 0] = mask_i
        aux_out[way, 1] = jnp.where(west_id >= 0, take_rows(place, west_at), -1)
        aux_out[way, 2] = jnp.where(east_id >= 0, take_rows(place, east_at), -1)

    for way, other, there in ways[::-1]:

        @pl.when(there)
        def _():
            aux_copy(way, other).start()

    @pl.when(tile > 0)
    def _():
        start_halos(0)

    for lf in range(1, nf):
        start_halos(lf)

    for way, other, there in ways:

        @pl.when(jnp.logical_not(comes[way]))
        def _():
            aux_in[way] = jnp.zeros(aux_in.shape[1:], jnp.int32)
            for lf in range(nf):
                run = pl.ds(lf * NDIR + way * half, half)
                halo[run] = jnp.zeros((half,) + shape, jnp.float32)

    mask = mask_i.astype(jnp.float32)
    one = jnp.float32(1.0)
    zero = jnp.float32(0.0)
    empty = jnp.zeros(shape, jnp.float32)
    ratio_spec = table_pick(spec, [1.1 ** (nf * s) for s in range(ns)])
    ratio_of = [ratio_spec * jnp.float32(1.1**lf) for lf in range(nf)]

    def sideways(at, valid, edge):
        return (
            jnp.where(col_of == edge, at, sublane),
            jnp.where((col_of == COLS - 1 - edge) & jnp.logical_not(valid), zero, one),
        )

    lanes_of = (
        row_of * COLS + lax.rem(col_of + COLS - 1, COLS),
        row_of * COLS + lax.rem(col_of + 1, COLS),
    )
    side_own = (
        sideways(west_at, west_id >= 0, COLS - 1),
        sideways(east_at, east_id >= 0, 0),
    )
    def halo_tables(way):
        place, ident, turn = (
            (north_at, north_id, POINTS - COLS), (south_at, south_id, COLS)
        )[way]

        @pl.when(comes[way])
        def _():
            aux_copy(way, ways[way][1]).wait_recv()

        factor_t[way, 4] = jnp.where(ident >= 0, take_rows(aux_in[way, 0], place), 0).astype(
            jnp.float32
        )
        index_t[way, 6] = place
        index_t[way, 7] = lax.rem(lane + turn, POINTS)
        for q in range(2):
            side = way if q == 0 else 1 - way
            pull, keep = side_own[side]
            at = take_rows(aux_in[way, 1 + side], place)
            hpull, hkeep = sideways(jnp.maximum(at, 0), at >= 0, COLS - 1 if side == 0 else 0)
            index_t[way, q], index_t[way, 2 + q], index_t[way, 4 + q] = pull, hpull, lanes_of[side]
            factor_t[way, q], factor_t[way, 2 + q] = keep, hkeep

    chunk = NDIR // 3
    order = sorted(range(1, ns), key=lambda k: -min(k // 2, (ns - k) // 2))

    def peer(k):
        return lax.rem(spec + k, ns)

    def share_copy(lf, k, d=0, count=NDIR):
        return pltpu.make_async_remote_copy(
            src_ref=own.at[pl.ds(lf * NDIR + d, count), peer(k)],
            dst_ref=gathered.at[pl.ds(d, count), lf * ns + spec],
            send_sem=share_send.at[lf], recv_sem=share_recv.at[lf],
            device_id={"spec": peer(k)}, device_id_type=MESH,
        )

    def share_local(lf):
        return pltpu.make_async_copy(
            own.at[pl.ds(lf * NDIR, NDIR), spec], gathered.at[:, lf * ns + spec], share_own.at[lf]
        )

    def share_all(sem):
        return pltpu.make_async_copy(
            gathered.at[:, pl.ds(0, ns - 1)], gathered.at[:, pl.ds(ns, ns - 1)], sem
        )

    def q_all(sem):
        return pltpu.make_async_copy(
            q_in.at[:, pl.ds(0, ns - 1)], q_in.at[:, pl.ds(0, ns - 1)], sem
        )

    def q_copy(k):
        return pltpu.make_async_remote_copy(
            src_ref=q_out.at[pl.ds(0, SOURCE_ITERS)], dst_ref=q_in.at[:, spec],
            send_sem=q_send.at[0], recv_sem=q_recv.at[0],
            device_id={"spec": peer(k)}, device_id_type=MESH,
        )

    swap = (tile > 0).astype(jnp.int32)
    edge = (tile <= 1) | (tile == nt - 1)

    def advance(group, carry):
        lf = jnp.where(edge, lax.rem(group, nf), group // 2)
        way = jnp.where(edge, lax.rem(group // nf + swap, 2), lax.rem(group + swap, 2))
        opens = jnp.where(edge, group < nf, lax.rem(group, 2) == 0)
        ratio = jnp.float32(ratio_of[0])
        for k in range(1, nf):
            ratio = jnp.where(lf == k, ratio_of[k], ratio)
        speed = jnp.float32(0.65) / ratio
        start = lf * NDIR + way * half

        @pl.when(opens)
        def _():
            own_copy(lf).wait()

        for w in range(2):

            @pl.when((way == w) & (lf == 0))
            def _():
                halo_tables(w)

            @pl.when((way == w) & comes[w])
            def _():
                halo_copy(lf, w, ways[w][1]).wait_recv()

        rim = row_of == (ROWS - 1) * (1 - way)
        place, turned = index_t[way, 6], index_t[way, 7]
        hmask = factor_t[way, 4]
        xs = [own[start + i] * mask for i in range(half)]
        hs = [take_rows(halo[start + i], place) * hmask for i in range(half)]
        coefs = []
        for i in range(half):
            ax = speed * jnp.float32(abs(math.cos(ANGLE[i])))
            ay = speed * jnp.float32(abs(math.sin(ANGLE[i])))
            coefs.append((ax, ay, one - ax - ay))
        for step in range(SUBSTEPS):
            for i in range(half):
                q = i // QUAD
                ax, ay, rest = coefs[i]
                lanes = index_t[way, 4 + q]
                x, h = xs[i], hs[i]
                side_x = take_lanes(take_rows(x, index_t[way, q]), lanes)
                side_y = take_lanes(jnp.where(rim, h, x), turned)
                xs[i] = (rest * x + (ax * factor_t[way, q]) * side_x + ay * side_y) * mask
                if step < SUBSTEPS - 1:
                    side_x = take_lanes(take_rows(h, index_t[way, 2 + q]), lanes)
                    side_y = take_lanes(h, turned)
                    hs[i] = (rest * h + (ax * factor_t[way, 2 + q]) * side_x + ay * side_y) * hmask
        for i in range(half):
            own[start + i] = xs[i]

        @pl.when(group == jnp.where(edge, 0, 1))
        def _():
            pl.semaphore_wait(met, len(greeted))

        @pl.when(edge)
        def _():
            for k in order:
                share_copy(lf, k, way * half, half).start()

        @pl.when(jnp.logical_not(edge | opens))
        def _():
            for k in order:
                share_copy(lf, k).start()

        @pl.when(jnp.logical_not(opens))
        def _():
            share_local(lf).start()

        return carry

    lax.fori_loop(0, 2 * nf, advance, 0)

    small[2].wait()
    small[3].wait()
    scaled = small_f[0] * jnp.float32(0.2 * 0.03)
    small_f[2] = jnp.cos(small_f[1])
    small_f[3] = jnp.sin(small_f[1])
    small_f[4] = mask_i.astype(jnp.float32)
    small_f[5] = scaled

    def mine(k):
        return jnp.broadcast_to(small_f[k, pl.ds(spec, 1), :], (8, POINTS))

    for target, cos_w, sin_w, scale in (
        (grow, small_f[2], small_f[3], scaled), (grow_row, mine(2), mine(3), mine(5))
    ):
        along, across = scale * cos_w, scale * sin_w
        for d in range(QUAD):
            cos_d, sin_d = jnp.float32(math.cos(ANGLE[d])), jnp.float32(math.sin(ANGLE[d]))
            ahead = along * cos_d + across * sin_d
            aside = across * cos_d - along * sin_d
            target[d] = jnp.maximum(ahead, 0.0)
            target[QUAD + d] = jnp.maximum(aside, 0.0)
            target[2 * QUAD + d] = jnp.maximum(-ahead, 0.0)
            target[3 * QUAD + d] = jnp.maximum(-aside, 0.0)

    mask_row = mine(4)
    place8 = lax.broadcasted_iota(jnp.int32, (8, POINTS), 0)
    empty8 = jnp.zeros((8, POINTS), jnp.float32)
    freqs = [table_rows(place8, [1.1 ** (nf * s + b) for s in range(ns)]) for b in range(blocks)]
    freq_root = [
        table_rows(place8, [math.sqrt(1.1 ** (nf * s + b)) for s in range(ns)]) for b in range(blocks)
    ]
    freq_limit = [jnp.float32(0.08) / ratio for ratio in freqs]

    sums = []
    for b in range(blocks):
        share_local(b).wait()
        share_all(share_recv.at[b]).wait()
        parts = [empty8] * 4
        for d in range(NDIR):
            parts[d % 4] = parts[d % 4] + gathered[d, 8 * b : 8 * b + 8, :]
        sums.append((parts[0] + parts[1]) + (parts[2] + parts[3]))
    for step in range(SOURCE_ITERS):
        first = sum(ratio * t for ratio, t in zip(freqs, sums))
        second = sum(ratio * ratio * t for ratio, t in zip(freqs, sums))
        first = jnp.sum(first, axis=0, keepdims=True) * jnp.float32(1.0 / total_comps)
        second = jnp.sum(second, axis=0, keepdims=True) * jnp.float32(1.0 / total_comps)
        mean_ratio = (second + 0.1) / (first + 0.1)
        damping = jnp.float32(0.2 * 0.25) * first / (mean_ratio * mean_ratio)
        q_out[step : step + 1, :] = damping
        if step == SOURCE_ITERS - 1:
            break
        damping = jnp.broadcast_to(damping, (8, POINTS))
        damp = [damping * (ratio * ratio) for ratio in freqs]

        def relax(j, sums):
            sums = list(sums)
            for i in range(chunk):
                d = j * chunk + i
                g = grow_row[d]
                for b in range(blocks):
                    x = gathered[d, 8 * b : 8 * b + 8, :]
                    change = (g * freq_root[b] - damp[b]) * x
                    change = jnp.minimum(jnp.maximum(change, -freq_limit[b]), freq_limit[b])
                    x = jnp.maximum(x + change, 0.0) * mask_row
                    gathered[d, 8 * b : 8 * b + 8, :] = x
                    sums[b] = sums[b] + x
            return tuple(sums)

        sums = lax.fori_loop(0, NDIR // chunk, relax, (empty8,) * blocks)

    for k in order:
        q_copy(k).start()
    q_in[:, pl.ds(spec, 1), :] = q_out[0:SOURCE_ITERS, :].reshape(SOURCE_ITERS, 1, POINTS)
    root_spec = table_pick(spec, [math.sqrt(1.1 ** (nf * s)) for s in range(ns)])
    root = [root_spec * jnp.float32(math.sqrt(1.1**lf)) for lf in range(nf)]
    limit = [jnp.float32(0.08) / ratio for ratio in ratio_of]
    for lf in range(nf):
        share_all(share_send.at[lf]).wait()
    q_all(q_recv.at[0]).wait()
    dampings = [q_in[step] for step in range(SOURCE_ITERS)]
    damps = [[t * (ratio * ratio) for ratio in ratio_of] for t in dampings]

    def settle(j, carry):
        for i in range(chunk):
            d = j * chunk + i
            g = grow[d]
            for lf in range(nf):
                x = own[lf * NDIR + d]
                gain = g * root[lf]
                for step in range(SOURCE_ITERS):
                    change = (gain - damps[step][lf]) * x
                    change = jnp.minimum(jnp.maximum(change, -limit[lf]), limit[lf])
                    x = jnp.maximum(x + change, 0.0) * mask
                own[lf * NDIR + d] = x
        return carry

    lax.fori_loop(0, NDIR // chunk, settle, 0)

    for way, other, there in ways:

        @pl.when(there)
        def _():
            aux_copy(way, other).wait_send()
            pltpu.make_async_copy(
                halo.at[pl.ds(0, nf * half)], halo.at[pl.ds(nf * half, nf * half)], halo_send.at[way]
            ).wait()

    q_all(q_send.at[0]).wait()


def body(nt, ns, spectra, wind_speed, wind_dir, sea_mask, neighbours):
    comps, tiles_dev, points = spectra.shape
    nf = comps // NDIR
    anywhere = pl.BlockSpec(memory_space=pl.ANY)
    dma = pltpu.SemaphoreType.DMA
    operands = [
        pltpu.with_memory_space_constraint(x, pltpu.HBM)
        for x in (spectra, wind_speed, wind_dir, sea_mask, neighbours.T)
    ]
    return pl.pallas_call(
        functools.partial(kernel, nt, ns, nf),
        out_shape=pltpu.VMEM(spectra.shape, jnp.float32),
        in_specs=[anywhere] * 5,
        out_specs=pl.BlockSpec(memory_space=pltpu.VMEM),
        scratch_shapes=[
            pltpu.VMEM((comps, tiles_dev, points), jnp.float32),
            pltpu.SMEM((4, tiles_dev), jnp.int32),
            pltpu.VMEM((6, tiles_dev, points), jnp.float32),
            pltpu.VMEM((tiles_dev, points), jnp.int32),
            pltpu.VMEM((2, 3, tiles_dev, points), jnp.int32),
            pltpu.VMEM((2, 3, tiles_dev, points), jnp.int32),
            pltpu.VMEM((NDIR, tiles_dev, points), jnp.float32),
            pltpu.VMEM((NDIR, 8, points), jnp.float32),
            pltpu.VMEM((NDIR, nf * ns, points), jnp.float32),
            pltpu.VMEM((8, points), jnp.float32),
            pltpu.VMEM((SOURCE_ITERS, tiles_dev, points), jnp.float32),
            pltpu.VMEM((2, 8, tiles_dev, points), jnp.int32),
            pltpu.VMEM((2, 5, tiles_dev, points), jnp.float32),
            dma((nf,)),
            dma((4,)),
            dma((2,)),
            dma((2,)),
            dma((2,)),
            dma((nf, 2)),
            dma((nf,)),
            dma((nf,)),
            dma((nf,)),
            dma((1,)),
            dma((1,)),
            pltpu.SemaphoreType.REGULAR,
        ],
        compiler_params=pltpu.CompilerParams(
            collective_id=0, has_side_effects=True, vmem_limit_bytes=16 * 1024 * 1024
        ),
    )(*operands)


def solution(mesh):
    placed = (
        P("spec", "tile", None),
        P("tile", None),
        P("tile", None),
        P("tile", None),
        P("tile", None),
    )
    return jax.shard_map(
        functools.partial(body, mesh.shape["tile"], mesh.shape["spec"]),
        mesh=mesh, in_specs=placed, out_specs=P("spec", "tile", None), check_vma=False,
    )
```
